512 devices in a mesh: lat: 16 (over z_hi, x), lon: 32 (over z_lo, y, core).
Axes of the slice: x: 4, y: 8, z: 8 (z_hi: 4, z_lo: 2; z = z_hi * 2 + z_lo), core: 2. Of those that a mesh axis runs over, the one named last changes fastest.
Arguments:
- tokens: bfloat16 [192, 768, 2, 512], P('lat', 'lon'), may hold values from -6 to 6
- gain_down: float32 [512], replicated, may hold values from 0.1 to 1.9
- qkv_down: bfloat16 [512, 768], replicated, may hold values from -0.25 to 0.25
- out_down: bfloat16 [256, 512], replicated, may hold values from -0.375 to 0.375
- merge_gain: float32 [2048], replicated, may hold values from 0.1 to 1.9
- merge_weight: bfloat16 [2048, 1024], P('lon'), may hold values from -0.125 to 0.125
- gain_mid: float32 [1024], replicated, may hold values from 0.1 to 1.9
- qkv_mid: bfloat16 [1024, 1536], P('lon'), may hold values from -0.1875 to 0.1875
- out_mid: bfloat16 [512, 1024], P('lon'), may hold values from -0.25 to 0.25
- expand_weight: bfloat16 [1024, 2048], P('lon'), may hold values from -0.1875 to 0.1875
- gain_up: float32 [512], replicated, may hold values from 0.1 to 1.9
- qkv_up: bfloat16 [512, 768], replicated, may hold values from -0.25 to 0.25
- out_up: bfloat16 [256, 512], replicated, may hold values from -0.375 to 0.375
Outputs:
- decoded: bfloat16 [192, 768, 2, 512], P('lat', 'lon')
The draws below stay inside these ranges and needn't reach their ends.
All inputs are finite; a program needn't handle non-finite values.
Results may differ from the reference program's by a relative error of at most 0.02.
Values may be sent and summed in bfloat16 or wider, within the bound.
A program may use at most 128 MiB of HBM per device.

```python
import jax
import jax.numpy as jnp
from jax import lax

C1 = 512
C2 = 1024
HD = 64
H1 = 4
H2 = 8
WA = 6
WO = 12
LV = 2
NLAT = 192
NLON = 768


def steps_of(key, shape, pieces, smallest, top_value):
    def one(position, blocks):
        steps = jax.random.uniform(jax.random.fold_in(jax.random.fold_in(key, 6), position), (blocks,), jnp.float32, smallest / len(pieces), top_value / len(pieces))
        return jnp.repeat(jnp.exp(steps), shape[position] // blocks).reshape((-1,) + (1,) * (len(shape) - position - 1))

    factor_of = one(*pieces[0])
    for cut in pieces[1:]:
        factor_of = factor_of * one(*cut)
    return factor_of


def centred(own_key, shape, scale, reach, shards=(), held_as=jnp.bfloat16):
    entries = scale * jax.random.normal(own_key, shape, jnp.float32)
    if shards:
        entries = entries * steps_of(own_key, shape, shards, -0.22, 0.18)
    return jnp.clip(entries, -reach, reach).astype(held_as)


def setup_inputs(seed: int = 0) -> dict:
    seeds = jax.random.split(jax.random.key(seed), 14)
    tokens = centred(seeds[0], (NLAT, NLON, LV, C1), 1.0, 6.0, ((0, 16), (1, 32)))
    gain_down = jnp.clip(1.0 + 0.18 * jax.random.normal(seeds[1], (C1,), jnp.float32), 0.1, 1.9)
    qkv_down = centred(seeds[2], (C1, 3 * H1 * HD), C1 ** -0.5, 0.25)
    out_down = centred(seeds[3], (H1 * HD, C1), (H1 * HD) ** -0.5, 0.375)
    merge_gain = jnp.clip(1.0 + 0.18 * jax.random.normal(seeds[4], (4 * C1,), jnp.float32), 0.1, 1.9)
    merge_weight = centred(seeds[5], (4 * C1, C2), (4 * C1) ** -0.5, 0.125, ((0, 32),))
    gain_mid = jnp.clip(1.0 + 0.18 * jax.random.normal(seeds[6], (C2,), jnp.float32), 0.1, 1.9)
    qkv_mid = centred(seeds[7], (C2, 3 * H2 * HD), C2 ** -0.5, 0.1875, ((0, 32),))
    out_mid = centred(seeds[8], (H2 * HD, C2), (H2 * HD) ** -0.5, 0.25, ((0, 32),))
    expand_weight = centred(seeds[9], (C2, 4 * C1), C2 ** -0.5, 0.1875, ((0, 32),))
    gain_up = jnp.clip(1.0 + 0.18 * jax.random.normal(seeds[10], (C1,), jnp.float32), 0.1, 1.9)
    qkv_up = centred(seeds[11], (C1, 3 * H1 * HD), C1 ** -0.5, 0.25)
    out_up = centred(seeds[12], (H1 * HD, C1), (H1 * HD) ** -0.5, 0.375)
    return dict(tokens=tokens, gain_down=gain_down, qkv_down=qkv_down, out_down=out_down, merge_gain=merge_gain, merge_weight=merge_weight, gain_mid=gain_mid, qkv_mid=qkv_mid, out_mid=out_mid, expand_weight=expand_weight, gain_up=gain_up, qkv_up=qkv_up, out_up=out_up)


def normalize(inputs, scales):
    values = inputs.astype(jnp.float32)
    center = lax.optimization_barrier(jnp.mean(values, axis=-1, keepdims=True))
    spread = lax.optimization_barrier(jnp.mean((values - center) ** 2, axis=-1, keepdims=True))
    return ((values - center) * lax.rsqrt(spread + 1e-05) * scales).astype(jnp.bfloat16)

def to_windows(tensor, head_count):
    row_count, col_count, level_count, feat_count = tensor.shape
    tensor = tensor.reshape(row_count // WA, WA, col_count // WO, WO, level_count, head_count, feat_count // head_count)
    tensor = tensor.transpose(0, 2, 1, 3, 4, 5, 6)
    return tensor.reshape(row_count // WA * (col_count // WO), WA * WO * level_count, head_count, feat_count // head_count)

def from_windows(tensor, row_count, col_count, level_count):
    feat_count = tensor.shape[2] * tensor.shape[3]
    tensor = tensor.reshape(row_count // WA, col_count // WO, WA, WO, level_count, feat_count)
    return tensor.transpose(0, 2, 1, 3, 4, 5).reshape(row_count, col_count, level_count, feat_count)

def window_attention(queries, keys_vals, row_valid, head_count):
    row_count, col_count, level_count, inner = queries.shape
    query_w = to_windows(queries, head_count).astype(jnp.float32)
    key_w = to_windows(keys_vals[..., :inner], head_count).astype(jnp.float32)
    value_w = to_windows(keys_vals[..., inner:], head_count).astype(jnp.float32)
    valid_full = jnp.broadcast_to(row_valid[:, None, None, None], (row_count, col_count, level_count, 1)).astype(jnp.float32)
    key_valid = to_windows(valid_full, 1)[:, :, 0, 0]
    score_scale = query_w.shape[3] ** (-0.5)
    scores = jnp.einsum('wphd,wqhd->whpq', query_w, key_w) * score_scale
    scores = jnp.where(key_valid[:, None, None, :] > 0.5, scores, -1e+30)
    attn_prob = jax.nn.softmax(scores, axis=-1).astype(jnp.bfloat16)
    context = jnp.einsum('whpq,wqhd->wphd', attn_prob.astype(jnp.float32), value_w).astype(jnp.bfloat16)
    return from_windows(context, row_count, col_count, level_count)

def attend_all(queries, keys_vals, row_valid, head_count):
    row_count = queries.shape[0]

    def row_window(window_row):
        offset = window_row * WA
        query_rows = lax.dynamic_slice_in_dim(queries, offset, WA, 0)
        kv_rows = lax.dynamic_slice_in_dim(keys_vals, offset, WA, 0)
        valid_rows = lax.dynamic_slice_in_dim(row_valid, offset, WA, 0)
        return window_attention(query_rows, kv_rows, valid_rows, head_count)
    stacked = lax.map(row_window, jnp.arange(row_count // WA, dtype=jnp.int32))
    return stacked.reshape((row_count,) + stacked.shape[2:])

def swin_block(inputs, scales, w_qkv, w_out, head_count):
    row_count, col_count, level_count, feat_count = inputs.shape
    normed = normalize(inputs, scales).reshape(-1, feat_count)
    projected = jnp.dot(normed, w_qkv, preferred_element_type=jnp.float32).astype(jnp.bfloat16)
    projected = projected.reshape(row_count, col_count, level_count, -1)
    inner = projected.shape[3] // 3
    half_lat = WA // 2
    half_lon = WO // 2
    padded = jnp.pad(projected, ((half_lat, half_lat), (0, 0), (0, 0), (0, 0)))
    rolled = jnp.roll(padded, half_lon, axis=1)
    row_index = jnp.arange(row_count + WA, dtype=jnp.int32)
    row_valid = (row_index >= half_lat) & (row_index < row_count + half_lat)
    attended = attend_all(rolled[..., :inner], rolled[..., inner:], row_valid, head_count)
    attended = jnp.roll(attended, -half_lon, axis=1)[half_lat:half_lat + row_count]
    out_proj = jnp.dot(attended.reshape(-1, inner), w_out, preferred_element_type=jnp.float32)
    return (inputs.astype(jnp.float32) + out_proj.reshape(inputs.shape)).astype(jnp.bfloat16)

def reference(tokens, gain_down, qkv_down, out_down, merge_gain, merge_weight, gain_mid, qkv_mid, out_mid, expand_weight, gain_up, qkv_up, out_up):
    fine_out = swin_block(tokens, gain_down, qkv_down, out_down, H1)
    row_count, col_count, level_count, feat_count = fine_out.shape
    merged = fine_out.reshape(row_count // 2, 2, col_count // 2, 2, level_count, feat_count)
    merged = merged.transpose(0, 2, 4, 3, 1, 5).reshape(-1, 4 * feat_count)
    normed = normalize(merged, merge_gain)
    coarse_in = jnp.dot(normed, merge_weight, preferred_element_type=jnp.float32).astype(jnp.bfloat16)
    coarse_in = coarse_in.reshape(row_count // 2, col_count // 2, level_count, -1)
    coarse_out = swin_block(coarse_in, gain_mid, qkv_mid, out_mid, H2)
    expanded = jnp.dot(coarse_out.reshape(-1, coarse_out.shape[3]), expand_weight, preferred_element_type=jnp.float32)
    expanded = expanded.reshape(row_count // 2, col_count // 2, level_count, 2, 2, feat_count)
    expanded = expanded.transpose(0, 4, 1, 3, 2, 5).reshape(row_count, col_count, level_count, feat_count)
    joined = (expanded + fine_out.astype(jnp.float32)).astype(jnp.bfloat16)
    return swin_block(joined, gain_up, qkv_up, out_up, H1)
```

```python
import functools
import jax
import jax.numpy as jnp
from jax import lax
from jax.experimental import pallas as pl
from jax.experimental.pallas import tpu as pltpu
from jax.sharding import PartitionSpec as P

MESH = pl.DeviceIdType.MESH


def places():
    lat, lon = lax.axis_index("lat"), lax.axis_index("lon")
    lats = lax.axis_size("lat")
    core = lon % 2
    y = (lon // 2) % 8
    plane = lon // 16
    at = lambda p, yy: p * 16 + ((yy + 16) % 8) * 2 + core
    return dict(
        lat=lat, lon=lon, core=core, y=y, plane=plane, at=at,
        up=(lat, at(plane, y + 1)),
        down=(lat, at(plane, y - 1)),
        above=((lat + 4 * plane) % lats, at(1 - plane, y)),
        below=((lat + 4 * plane + lats - 4) % lats, at(1 - plane, y)),
        twin=(lat, lon + 1 - 2 * core),
    )


class Gather:
    def __init__(self, here, own, full, ring, cross, twin, sent, local):
        self.here, self.own, self.full = here, own, full
        self.ring, self.cross, self.twin, self.sent, self.local = ring, cross, twin, sent, local
        self.half = full.shape[2] // 2

    def push(self, src, dst, sem, to):
        pltpu.make_async_remote_copy(
            src_ref=src, dst_ref=dst, send_sem=self.sent, recv_sem=sem,
            device_id=to, device_id_type=MESH,
        ).start()

    def block(self, index, half=None):
        if half is None:
            return self.full.at[index]
        return self.full.at[index, :, pl.ds(half * self.half, self.half)]

    def move(self, index, sem, to, half=None):
        self.push(self.block(index, half), self.block(index, half), sem, to)

    def await_blocks(self, sem, count):
        view = self.full.at[pl.ds(0, count)]
        pltpu.make_async_copy(view, view, sem).wait()

    def phase(self, k):
        h = self.here
        me, at, y, plane = h["lon"], h["at"], h["y"], h["plane"]
        if k == 0:
            for to in ("up", "down"):
                self.push(self.own, self.block(me), self.ring.at[0], h[to])
            for half, to in enumerate(("above", "below")):
                cols = pl.ds(half * self.half, self.half)
                self.push(self.own.at[:, cols], self.block(me, half), self.cross.at[0], h[to])
            self.push(self.own, self.block(me), self.twin, h["twin"])
            pltpu.make_async_copy(self.own, self.block(me), self.local).start()
            return
        if k <= 3:
            self.await_blocks(self.ring.at[k - 1], 2)
            got_up, got_down = at(plane, y - k), at(plane, y + k)
            self.move(got_up, self.ring.at[k], h["up"], 0 if k == 3 else None)
            self.move(got_down, self.ring.at[k], h["down"], 1 if k == 3 else None)
            for index in (got_up, got_down):
                self.move(index, self.cross.at[k], h["above"], 0)
                self.move(index, self.cross.at[k], h["below"], 1)
            for index in (got_up, got_down):
                self.move(index, self.twin, h["twin"])
        if k == 4:
            self.await_blocks(self.ring.at[3], 1)
            far = at(plane, y + 4)
            self.move(far, self.cross.at[4], h["above"], 0)
            self.move(far, self.cross.at[4], h["below"], 1)
            self.move(far, self.twin, h["twin"])
        if k in (1, 5):
            self.await_blocks(self.cross.at[k - 1], 1)
            self.move(at(1 - plane, y + k - 1), self.twin, h["twin"])
        else:
            self.await_blocks(self.cross.at[k - 1], 2)
            for yy in (y - k + 1, y + k - 1):
                self.move(at(1 - plane, yy), self.twin, h["twin"])

    def settle(self):
        self.await_blocks(self.twin, 16)
        pltpu.make_async_copy(self.own, self.block(self.here["lon"]), self.local).wait()

    def finish(self):
        self.await_blocks(self.sent, 31)


def gather_kernel(*refs):
    owns, fulls = refs[:4], refs[4:8]
    ring, cross, twin, sent, local = refs[8:]
    here = places()
    barrier = pltpu.get_barrier_semaphore()
    for to in ("up", "down", "above", "below", "twin"):
        pl.semaphore_signal(barrier, inc=1, device_id=here[to], device_id_type=MESH)
    pl.semaphore_wait(barrier, 5)
    gathers = [
        Gather(here, owns[i], fulls[i], ring.at[i], cross.at[i], twin.at[i], sent.at[i], local.at[i])
        for i in range(4)
    ]
    for slot in range(6 + 3):
        for i, g in enumerate(gathers):
            if 0 <= slot - i < 6:
                g.phase(slot - i)
    for g in gathers:
        g.settle()
    for g in gathers:
        g.finish()


def gather_weights(weights):
    shapes = [jax.ShapeDtypeStruct((32,) + w.shape, w.dtype) for w in weights]
    return pl.pallas_call(
        gather_kernel,
        out_shape=shapes,
        in_specs=[pl.BlockSpec(memory_space=pl.ANY)] * 4,
        out_specs=[pl.BlockSpec(memory_space=pltpu.VMEM)] * 4,
        scratch_shapes=[
            pltpu.SemaphoreType.DMA((4, 4)),
            pltpu.SemaphoreType.DMA((4, 5)),
            pltpu.SemaphoreType.DMA((4,)),
            pltpu.SemaphoreType.DMA((4,)),
            pltpu.SemaphoreType.DMA((4,)),
        ],
        compiler_params=pltpu.CompilerParams(
            collective_id=0, has_side_effects=True, vmem_limit_bytes=40 * 2**20
        ),
    )(*weights)


H1 = 4
H2 = 8
WA = 6
WO = 12


def extended(array, sides, width, wrap):
    for axis, dim in sides:
        count, length = (lax.axis_size(axis), array.shape[dim])
        up = [(i, (i + 1) % count) for i in range(count if wrap else count - 1)]
        down = [(j, i) for i, j in up]
        last = lax.slice_in_dim(array, length - width, length, axis=dim)
        leading = lax.slice_in_dim(array, 0, width, axis=dim)
        before = lax.ppermute(last, axis, up)
        after = lax.ppermute(leading, axis, down)
        array = jnp.concatenate([before, array, after], axis=dim)
    return array


def normalize(inputs, scales):
    values = inputs.astype(jnp.float32)
    center = jnp.mean(values, axis=-1, keepdims=True)
    spread = jnp.mean((values - center) ** 2, axis=-1, keepdims=True)
    return ((values - center) * lax.rsqrt(spread + 1e-05) * scales).astype(jnp.bfloat16)


def windows_of(tensor, row_size, col_size, head_count):
    row_count, col_count, level_count, feat_count = tensor.shape
    tensor = tensor.reshape(
        row_count // row_size,
        row_size,
        col_count // col_size,
        col_size,
        level_count,
        head_count,
        feat_count // head_count,
    )
    tensor = tensor.transpose(0, 2, 1, 3, 4, 5, 6)
    return tensor.reshape(
        row_count // row_size,
        col_count // col_size,
        row_size * col_size * level_count,
        head_count,
        feat_count // head_count,
    )


def doubled(tensor, axis):
    repeated = jnp.repeat(tensor, 2, axis=axis)
    return lax.slice_in_dim(repeated, 1, repeated.shape[axis] - 1, axis=axis)


def window_attention(queries, keys_vals, row_valid, head_count):
    row_count, col_count, level_count, inner = queries.shape
    half_lat = WA // 2
    half_lon = WO // 2
    query_w = windows_of(queries, half_lat, half_lon, head_count)
    key_w = doubled(doubled(windows_of(keys_vals[..., :inner], WA, WO, head_count), 0), 1)
    value_w = doubled(doubled(windows_of(keys_vals[..., inner:], WA, WO, head_count), 0), 1)
    valid_full = jnp.broadcast_to(
        row_valid[:, None, None, None], keys_vals.shape[:3] + (1,)
    ).astype(jnp.float32)
    key_valid = doubled(doubled(windows_of(valid_full, WA, WO, 1)[:, :, :, 0, 0], 0), 1)
    score_scale = query_w.shape[4] ** (-0.5)
    scores = (
        jnp.einsum("abphd,abqhd->abhpq", query_w, key_w, preferred_element_type=jnp.float32)
        * score_scale
    )
    scores = jnp.where(key_valid[:, :, None, None, :] > 0.5, scores, -1e30)
    attn_prob = jax.nn.softmax(scores, axis=-1).astype(jnp.bfloat16)
    context = jnp.einsum(
        "abhpq,abqhd->abphd", attn_prob, value_w, preferred_element_type=jnp.float32
    ).astype(jnp.bfloat16)
    context = context.reshape(
        row_count // half_lat, col_count // half_lon, half_lat, half_lon, level_count, inner
    )
    return context.transpose(0, 2, 1, 3, 4, 5).reshape(row_count, col_count, level_count, inner)


def project(inputs, weight, coarse):
    return jnp.dot(inputs, weight, preferred_element_type=jnp.float32)


def with_rims(keys_vals):
    lat_ext = extended(keys_vals, (("lat", 0),), WA // 2, False)
    return extended(lat_ext, (("lon", 1),), WO // 2, True)


def swin_block(inputs, scales, w_qkv, w_out, head_count, coarse):
    row_count, col_count, level_count, feat_count = inputs.shape
    normed = normalize(inputs, scales).reshape(-1, feat_count)
    projected = project(normed, w_qkv, coarse).astype(jnp.bfloat16)
    projected = projected.reshape(row_count, col_count, level_count, -1)
    inner = projected.shape[3] // 3
    keys_vals = with_rims(projected[..., inner:])
    half_lat = WA // 2
    global_row = (
        lax.axis_index("lat") * row_count - half_lat + jnp.arange(row_count + WA, dtype=jnp.int32)
    )
    row_valid = (global_row >= 0) & (global_row < row_count * lax.axis_size("lat"))
    attended = window_attention(projected[..., :inner], keys_vals, row_valid, head_count)
    out_proj = project(attended.reshape(-1, inner), w_out, coarse)
    return (inputs.astype(jnp.float32) + out_proj.reshape(inputs.shape)).astype(jnp.bfloat16)


def on_device(
    tokens,
    gain_down,
    qkv_down,
    out_down,
    merge_gain,
    merge_weight,
    gain_mid,
    qkv_mid,
    out_mid,
    expand_weight,
    gain_up,
    qkv_up,
    out_up,
):
    merge_weight, qkv_mid, out_mid, expand_weight = (
        full.reshape(-1, full.shape[2])
        for full in gather_weights((merge_weight, qkv_mid, out_mid, expand_weight))
    )
    fine_out = swin_block(tokens, gain_down, qkv_down, out_down, H1, False)
    row_count, col_count, level_count, feat_count = fine_out.shape
    merged = fine_out.reshape(row_count // 2, 2, col_count // 2, 2, level_count, feat_count)
    merged = merged.transpose(0, 2, 4, 3, 1, 5).reshape(-1, 4 * feat_count)
    normed = normalize(merged, merge_gain)
    coarse_in = project(normed, merge_weight, True).astype(jnp.bfloat16)
    coarse_in = coarse_in.reshape(row_count // 2, col_count // 2, level_count, -1)
    coarse_out = swin_block(coarse_in, gain_mid, qkv_mid, out_mid, H2, True)
    expanded = project(coarse_out.reshape(-1, coarse_out.shape[3]), expand_weight, True)
    expanded = expanded.reshape(row_count // 2, col_count // 2, level_count, 2, 2, feat_count)
    expanded = expanded.transpose(0, 4, 1, 3, 2, 5).reshape(
        row_count, col_count, level_count, feat_count
    )
    joined = (expanded + fine_out.astype(jnp.float32)).astype(jnp.bfloat16)
    return swin_block(joined, gain_up, qkv_up, out_up, H1, False)


def solution(mesh):
    return jax.shard_map(
        on_device,
        mesh=mesh,
        in_specs=(
            P("lat", "lon", None, None),
            P(),
            P(),
            P(),
            P(),
            P("lon", None),
            P(),
            P("lon", None),
            P("lon", None),
            P("lon", None),
            P(),
            P(),
            P(),
        ),
        out_specs=P("lat", "lon", None, None),
        check_vma=False,
    )
```

```python
import jax
import jax.numpy as jnp
import numpy as np
from jax import lax
from jax.experimental import pallas as pl
from jax.experimental.pallas import tpu as pltpu
from jax.sharding import PartitionSpec as P

MESH = pl.DeviceIdType.MESH


def places():
    lat, lon = lax.axis_index("lat"), lax.axis_index("lon")
    lats = lax.axis_size("lat")
    core = lon % 2
    y = (lon // 2) % 8
    plane = lon // 16
    at = lambda p, yy: p * 16 + ((yy + 16) % 8) * 2 + core
    offsets = [(a, b) for a in (-1, 0, 1) for b in (-1, 0, 1) if (a, b) != (0, 0)]
    return dict(
        north_pole=lat == 0, south_pole=lat == lats - 1,
        around={(a, b): ((lat + a + lats) % lats, (lon + b + 32) % 32) for a, b in offsets},
        lat=lat, lon=lon, core=core, y=y, plane=plane, at=at,
        up=(lat, at(plane, y + 1)),
        down=(lat, at(plane, y - 1)),
        above=((lat + 4 * plane) % lats, at(1 - plane, y)),
        below=((lat + 4 * plane + lats - 4) % lats, at(1 - plane, y)),
        twin=(lat, lon + 1 - 2 * core),
    )


class Gather:
    def __init__(self, here, own, full, ring, cross, twin, sent, local):
        self.here, self.own, self.full = here, own, full
        self.ring, self.cross, self.twin, self.sent, self.local = ring, cross, twin, sent, local
        self.half = full.shape[2] // 2

    def push(self, src, dst, sem, to):
        pltpu.make_async_remote_copy(
            src_ref=src, dst_ref=dst, send_sem=self.sent, recv_sem=sem,
            device_id=to, device_id_type=MESH,
        ).start()

    def block(self, index, half=None):
        if half is None:
            return self.full.at[index]
        return self.full.at[index, :, pl.ds(half * self.half, self.half)]

    def move(self, index, sem, to, half=None):
        self.push(self.block(index, half), self.block(index, half), sem, to)

    def await_blocks(self, sem, count):
        view = self.full.at[pl.ds(0, count)]
        pltpu.make_async_copy(view, view, sem).wait()

    def phase(self, k):
        h = self.here
        me, at, y, plane = h["lon"], h["at"], h["y"], h["plane"]
        if k == 0:
            for to in ("up", "down"):
                self.push(self.own, self.block(me), self.ring.at[0], h[to])
            for half, to in enumerate(("above", "below")):
                cols = pl.ds(half * self.half, self.half)
                self.push(self.own.at[:, cols], self.block(me, half), self.cross.at[0], h[to])
            self.push(self.own, self.block(me), self.twin, h["twin"])
            pltpu.make_async_copy(self.own, self.block(me), self.local).start()
            return
        if k <= 3:
            self.await_blocks(self.ring.at[k - 1], 2)
            got_up, got_down = at(plane, y - k), at(plane, y + k)
            self.move(got_up, self.ring.at[k], h["up"], 0 if k == 3 else None)
            self.move(got_down, self.ring.at[k], h["down"], 1 if k == 3 else None)
            for index in (got_up, got_down):
                self.move(index, self.cross.at[k], h["above"], 0)
                self.move(index, self.cross.at[k], h["below"], 1)
            for index in (got_up, got_down):
                self.move(index, self.twin, h["twin"])
        if k == 4:
            self.await_blocks(self.ring.at[3], 1)
            far = at(plane, y + 4)
            self.move(far, self.cross.at[4], h["above"], 0)
            self.move(far, self.cross.at[4], h["below"], 1)
            self.move(far, self.twin, h["twin"])
        if k in (1, 5):
            self.await_blocks(self.cross.at[k - 1], 1)
            self.move(at(1 - plane, y + k - 1), self.twin, h["twin"])
        else:
            self.await_blocks(self.cross.at[k - 1], 2)
            for yy in (y - k + 1, y + k - 1):
                self.move(at(1 - plane, yy), self.twin, h["twin"])

    def settle(self):
        self.await_blocks(self.twin, 16)
        pltpu.make_async_copy(self.own, self.block(self.here["lon"]), self.local).wait()

    def finish(self):
        self.await_blocks(self.sent, 31)


HEADS = 4
QB = 48
GROUP = 4 * 64


def quarter_order(rows, cols):
    place = -np.ones((rows // 3, cols // 6, QB, 3), np.int64)
    for i in range(rows // 3):
        for j in range(cols // 6):
            for k in range(36):
                place[i, j, k] = (3 * i + k // 12, 6 * j + k % 12 // 2, k % 2)
    return place.reshape(-1, 3)


def one_hot(index, width):
    out = np.zeros((len(index), width), np.float32)
    rows = np.arange(len(index))[index >= 0]
    out[rows, index[index >= 0]] = 1
    return out


def orders():
    fine = quarter_order(12, 24)
    coarse = quarter_order(6, 12)
    flat = np.where(fine[:, 0] < 0, -1, (fine[:, 0] * 24 + fine[:, 1]) * 2 + fine[:, 2])
    to_quarters = one_hot(flat, 576)
    slot = {tuple(p): n for n, p in enumerate(fine.tolist()) if p[0] >= 0}
    merge = []
    for k in range(4):
        for r, c, level in coarse.tolist():
            merge.append(-1 if r < 0 else slot[(2 * r + k % 2, 2 * c + k // 2, level)])
    to_merged = one_hot(np.array(merge), 16 * QB)
    as_bf16 = lambda a: jnp.asarray(a, jnp.bfloat16)
    return (as_bf16(to_quarters), as_bf16(to_quarters.T.copy()), as_bf16(to_merged), as_bf16(to_merged.T.copy()))


def dot(a, b):
    return jnp.dot(a, b, preferred_element_type=jnp.float32)


def normed(values, gain):
    center = jnp.mean(values, axis=-1, keepdims=True)
    away = values - center
    spread = jnp.mean(away * away, axis=-1, keepdims=True)
    return (away * lax.rsqrt(spread + 1e-05) * gain).astype(jnp.bfloat16)


def attend(q, k, v, bias):
    rows = q.shape[0]
    lane = lax.broadcasted_iota(jnp.int32, (1, GROUP), 1)
    of_head = [(lane >= 64 * h) & (lane < 64 * h + 64) for h in range(HEADS)]
    stacked = jnp.concatenate([jnp.where(m, q, jnp.zeros_like(q)) for m in of_head], axis=0)
    scores = lax.dot_general(stacked, k, (((1,), (1,)), ((), ())), preferred_element_type=jnp.float32)
    scores = scores + bias
    top = jnp.max(scores, axis=-1, keepdims=True)
    weights = jnp.exp(scores - top)
    total = jnp.sum(weights, axis=-1, keepdims=True)
    mixed = dot(weights.astype(jnp.bfloat16), v) / total
    out = mixed[:rows]
    for h in range(1, HEADS):
        out = jnp.where(of_head[h], mixed[h * rows : (h + 1) * rows], out)
    return out.astype(jnp.bfloat16)


def key_bias(first_hidden, second_hidden):
    lane = lax.broadcasted_iota(jnp.int32, (1, 4 * QB), 1)
    inner = lane
    for edge in (1, 2, 3):
        inner = inner - jnp.where(lane >= edge * QB, QB, 0)
    hidden = inner >= 36
    if first_hidden is not None:
        hidden = hidden | ((lane < 2 * QB) & first_hidden)
    if second_hidden is not None:
        hidden = hidden | ((lane >= 2 * QB) & second_hidden)
    return jnp.where(hidden, jnp.float32(-1e30), jnp.float32(0))


class Halo:
    def __init__(self, here, kv, send, recv):
        self.kv, self.send, self.recv = kv, send, recv
        n = kv.shape[0] - 2
        self.copies = []
        inner = {-1: pl.ds(1, 1), 0: pl.ds(1, n), 1: pl.ds(n, 1)}
        outer = {-1: pl.ds(n + 1, 1), 0: pl.ds(1, n), 1: pl.ds(0, 1)}
        for index, (a, b) in enumerate(here["around"]):
            self.copies.append(
                pltpu.make_async_remote_copy(
                    src_ref=kv.at[inner[a], inner[b]],
                    dst_ref=kv.at[outer[a], outer[b]],
                    send_sem=send.at[index],
                    recv_sem=recv.at[index],
                    device_id=here["around"][(a, b)],
                    device_id_type=MESH,
                )
            )

    def start(self):
        for copy in self.copies:
            copy.start()

    def wait(self):
        for copy in self.copies:
            copy.wait_recv()

    def finish(self):
        for copy in self.copies:
            copy.wait_send()


def window_rows(w, n):
    lo, hi = max(2 * w - 1, 0), min(2 * w + 1, n)
    return slice(lo, hi)


def attend_windows(here, q, kv, att, windows, groups):
    n = q.shape[0]
    inner = q.shape[3]
    last = n // 2
    for wi, wj in windows:
        bias = key_bias(
            here["north_pole"] if wi == 0 else None, here["south_pole"] if wi == last else None
        )
        rows, cols = window_rows(wi, n), window_rows(wj, n)
        for g in range(groups):
            lanes = slice(g * GROUP, g * GROUP + GROUP)
            vlanes = slice(inner + g * GROUP, inner + g * GROUP + GROUP)
            queries = q[rows, cols, :, lanes]
            shape = queries.shape
            out = attend(
                queries.reshape(-1, GROUP),
                kv[2 * wi : 2 * wi + 2, 2 * wj : 2 * wj + 2, :, lanes].reshape(-1, GROUP),
                kv[2 * wi : 2 * wi + 2, 2 * wj : 2 * wj + 2, :, vlanes].reshape(-1, GROUP),
                bias,
            )
            att[rows, cols, :, lanes] = out.reshape(shape)


def kernel(*refs):
    (tokens, gain_down, qkv_down, out_down, merge_gain, gain_mid, gain_up, qkv_up, out_up,
     to_quarters, from_quarters, to_merged, from_merged) = refs[:13]
    owns = refs[13:17]
    result = refs[17]
    fulls = refs[18:22]
    (x_down, kv_down, kv_up, q_fine, att_fine, fine_out, merged, x_mid, kv_mid, q_mid, att_mid,
     coarse_out, expanded, joined, decoded) = refs[22:37]
    ring, cross, twin, sent, local, halo_send, halo_recv = refs[37:]
    here = places()
    barrier = pltpu.get_barrier_semaphore()
    greeted = [here[to] for to in ("up", "down", "above", "below", "twin")]
    greeted += list(here["around"].values())
    for to in greeted:
        pl.semaphore_signal(barrier, inc=1, device_id=to, device_id_type=MESH)
    pl.semaphore_wait(barrier, len(greeted))
    gathers = [
        Gather(here, owns[i], fulls[i], ring.at[i], cross.at[i], twin.at[i], sent.at[i], local.at[i])
        for i in range(4)
    ]
    offsets = (0, 1, 2, 3)
    done = [0]

    def move():
        for i, g in enumerate(gathers):
            if 0 <= done[0] - offsets[i] < 6:
                g.phase(done[0] - offsets[i])
        done[0] += 1

    halos = [
        Halo(here, kv, halo_send.at[i], halo_recv.at[i])
        for i, kv in enumerate((kv_down, kv_mid, kv_up))
    ]

    def fine_project(i, n, w, kv):
        out = dot(n, w[...])
        q_fine[i] = (out[:, :256] * 0.125).astype(jnp.bfloat16).reshape(4, QB, 256)
        kv[1 + i, 1:5] = out[:, 256:].astype(jnp.bfloat16).reshape(4, QB, 512)

    def fine_output(i, x, w):
        rows = slice(192 * i, 192 * i + 192)
        branch = dot(att_fine[i].reshape(192, 256), w[...])
        return (x[rows].astype(jnp.float32) + branch).astype(jnp.bfloat16)

    rims = [(a, b) for a in range(3) for b in range(3) if (a, b) != (1, 1)]

    move()
    for i in (0, 3, 1, 2):
        rows = slice(192 * i, 192 * i + 192)
        x = dot(to_quarters[rows], tokens[...])
        x_down[rows] = x.astype(jnp.bfloat16)
        fine_project(i, normed(x, gain_down[...]), qkv_down, kv_down)
    halos[0].start()
    move()
    attend_windows(here, q_fine, kv_down, att_fine, [(1, 1)], 1)
    move()
    halos[0].wait()
    attend_windows(here, q_fine, kv_down, att_fine, rims[:4], 1)
    move()
    attend_windows(here, q_fine, kv_down, att_fine, rims[4:], 1)
    move()
    for i in range(4):
        fine_out[192 * i : 192 * i + 192] = fine_output(i, x_down, out_down)
    move()

    parts = [dot(to_merged[192 * k : 192 * k + 192], fine_out[...]) for k in range(4)]
    center = sum(jnp.sum(p, axis=-1, keepdims=True) for p in parts) * (1 / 2048)
    parts = [p - center for p in parts]
    spread = sum(jnp.sum(p * p, axis=-1, keepdims=True) for p in parts) * (1 / 2048)
    factor = lax.rsqrt(spread + 1e-05)
    for k in range(4):
        lanes = slice(512 * k, 512 * k + 512)
        merged[:, lanes] = (parts[k] * factor * merge_gain[:, lanes]).astype(jnp.bfloat16)
    move()
    gathers[0].settle()
    for c in range(4):
        lanes = slice(256 * c, 256 * c + 256)
        x_mid[:, lanes] = dot(merged[...], fulls[0][:, :, lanes].reshape(2048, 256)).astype(jnp.bfloat16)
    move()
    n_mid = normed(x_mid[...].astype(jnp.float32), gain_mid[...])
    gathers[1].settle()
    for c in range(6):
        out = dot(n_mid, fulls[1][:, :, 256 * c : 256 * c + 256].reshape(1024, 256))
        if c < 2:
            q_mid[:, :, :, 256 * c : 256 * c + 256] = (out * 0.125).astype(jnp.bfloat16).reshape(2, 2, QB, 256)
        else:
            lanes = slice(256 * (c - 2), 256 * (c - 1))
            kv_mid[1:3, 1:3, :, lanes] = out.astype(jnp.bfloat16).reshape(2, 2, QB, 256)
    halos[1].start()
    move()
    halos[1].wait()
    attend_windows(here, q_mid, kv_mid, att_mid, [(a, b) for a in range(2) for b in range(2)], 2)
    gathers[2].settle()
    for c in range(2):
        lanes = slice(512 * c, 512 * c + 512)
        out = dot(att_mid[...].reshape(192, 512), fulls[2][:, :, lanes].reshape(512, 512))
        coarse_out[:, lanes] = (x_mid[:, lanes].astype(jnp.float32) + out).astype(jnp.bfloat16)
    gathers[3].settle()
    for k in range(4):
        out = dot(coarse_out[...], fulls[3][:, :, 512 * k : 512 * k + 512].reshape(1024, 512))
        expanded[192 * k : 192 * k + 192] = out.astype(jnp.bfloat16)
    for i in (0, 3, 1, 2):
        rows = slice(192 * i, 192 * i + 192)
        x = dot(from_merged[rows], expanded[...]) + fine_out[rows].astype(jnp.float32)
        x = x.astype(jnp.bfloat16)
        joined[rows] = x
        fine_project(i, normed(x.astype(jnp.float32), gain_up[...]), qkv_up, kv_up)
    halos[2].start()
    attend_windows(here, q_fine, kv_up, att_fine, [(1, 1)], 1)
    halos[2].wait()
    attend_windows(here, q_fine, kv_up, att_fine, rims, 1)
    for i in range(4):
        decoded[192 * i : 192 * i + 192] = fine_output(i, joined, out_up)
    for i in range(4):
        rows = slice(144 * i, 144 * i + 144)
        result[rows] = dot(from_quarters[rows], decoded[...]).astype(jnp.bfloat16)
    for g in gathers:
        g.finish()
    for h in halos:
        h.finish()


def on_device(tokens, gain_down, qkv_down, out_down, merge_gain, merge_weight, gain_mid, qkv_mid,
              out_mid, expand_weight, gain_up, qkv_up, out_up):
    weights = (merge_weight, qkv_mid, out_mid, expand_weight)
    row = lambda g: g.reshape(1, -1)
    bf16 = jnp.bfloat16
    vmem = pl.BlockSpec(memory_space=pltpu.VMEM)
    out = pl.pallas_call(
        kernel,
        out_shape=jax.ShapeDtypeStruct((576, 512), bf16),
        in_specs=[vmem] * 13 + [pl.BlockSpec(memory_space=pl.ANY)] * 4,
        out_specs=vmem,
        scratch_shapes=[pltpu.VMEM((32,) + w.shape, w.dtype) for w in weights] + [
            pltpu.VMEM((768, 512), bf16),
            pltpu.VMEM((6, 6, QB, 512), bf16),
            pltpu.VMEM((6, 6, QB, 512), bf16),
            pltpu.VMEM((4, 4, QB, 256), bf16),
            pltpu.VMEM((4, 4, QB, 256), bf16),
            pltpu.VMEM((768, 512), bf16),
            pltpu.VMEM((192, 2048), bf16),
            pltpu.VMEM((192, 1024), bf16),
            pltpu.VMEM((4, 4, QB, 1024), bf16),
            pltpu.VMEM((2, 2, QB, 512), bf16),
            pltpu.VMEM((2, 2, QB, 512), bf16),
            pltpu.VMEM((192, 1024), bf16),
            pltpu.VMEM((768, 512), bf16),
            pltpu.VMEM((768, 512), bf16),
            pltpu.VMEM((768, 512), bf16),
            pltpu.SemaphoreType.DMA((4, 4)),
            pltpu.SemaphoreType.DMA((4, 5)),
            pltpu.SemaphoreType.DMA((4,)),
            pltpu.SemaphoreType.DMA((4,)),
            pltpu.SemaphoreType.DMA((4,)),
            pltpu.SemaphoreType.DMA((3, 8)),
            pltpu.SemaphoreType.DMA((3, 8)),
        ],
        compiler_params=pltpu.CompilerParams(
            collective_id=0, has_side_effects=True, vmem_limit_bytes=56 * 2**20
        ),
    )(tokens.reshape(576, 512), row(gain_down), qkv_down, out_down, row(merge_gain), row(gain_mid),
      row(gain_up), qkv_up, out_up, *orders(), *weights)
    return out.reshape(tokens.shape)


def solution(mesh):
    return jax.shard_map(
        on_device,
        mesh=mesh,
        in_specs=(
            P("lat", "lon", None, None), P(), P(), P(), P(), P("lon", None), P(), P("lon", None),
            P("lon", None), P("lon", None), P(), P(), P(),
        ),
        out_specs=P("lat", "lon", None, None),
        check_vma=False,
    )
```

```python
import jax
import jax.numpy as jnp
import numpy as np
from jax import lax
from jax.experimental import pallas as pl
from jax.experimental.pallas import tpu as pltpu
from jax.sharding import PartitionSpec as P

MESH = pl.DeviceIdType.MESH


def places():
    lat, lon = lax.axis_index("lat"), lax.axis_index("lon")
    lats = lax.axis_size("lat")
    core = lon % 2
    y = (lon // 2) % 8
    plane = lon // 16
    x = lat % 4
    at = lambda p, yy: p * 16 + ((yy + 16) % 8) * 2 + core
    return dict(
        north_pole=lat == 0, south_pole=lat == lats - 1,
        north=((lat + lats - 1) % lats, lon), south=((lat + 1) % lats, lon),
        west=(lat, (lon + 31) % 32), east=(lat, (lon + 1) % 32),
        lat=lat, lon=lon, core=core, x=x, y=y, plane=plane, at=at,
        up=(lat, at(plane, y + 1)),
        down=(lat, at(plane, y - 1)),
        above=((lat + 4 * plane) % lats, at(1 - plane, y)),
        below=((lat + 4 * plane + lats - 4) % lats, at(1 - plane, y)),
        right=(lat - x + (x + 1) % 4, lon),
        left=(lat - x + (x + 3) % 4, lon),
        twin=(lat, lon + 1 - 2 * core),
    )


WHOLE, FOURTH = 1024, 256


class Gather:
    def __init__(self, here, groups, near, far, ring, cross, side, second, twin, sent, local):
        self.here, self.groups, self.near, self.far = here, groups, near, far
        self.ring, self.cross, self.side, self.second = ring, cross, side, second
        self.twin, self.sent, self.local = twin, sent, local

    def push(self, src, dst, sem, to, kind=0):
        pltpu.make_async_remote_copy(
            src_ref=src, dst_ref=dst, send_sem=self.sent.at[kind], recv_sem=sem,
            device_id=self.here[to], device_id_type=MESH,
        ).start()

    def await_near(self, sem, count):
        view = self.near.at[self.groups, pl.ds(0, count)]
        pltpu.make_async_copy(view, view, sem).wait()

    def await_far(self, sem, count, fourths):
        view = self.far.at[self.groups, pl.ds(0, count), :, pl.ds(0, fourths * FOURTH)]
        pltpu.make_async_copy(view, view, sem).wait()

    def block(self, index, half=None):
        rows = slice(None) if half is None else pl.ds(16 * half, 16)
        return self.near.at[self.groups, index, rows]

    def fourth(self, index, distance, half=None):
        rows = slice(None) if half is None else pl.ds(16 * half, 16)
        if distance == 0:
            return self.near.at[self.groups, index, rows, pl.ds(WHOLE, FOURTH)]
        return self.far.at[self.groups, index, rows, pl.ds((distance - 1) * FOURTH, FOURTH)]

    def move(self, index, sem, to, half=None):
        self.push(self.block(index, half), self.block(index, half), sem, to)

    def batch(self, plane, k):
        at, y = self.here["at"], self.here["y"]
        p = self.here["plane"] if plane == 0 else 1 - self.here["plane"]
        return [at(p, y + k)] if k in (0, 4) else [at(p, y - k), at(p, y + k)]

    def spread(self, plane, k):
        blocks = self.batch(plane, k)
        if (plane, k) != (0, 0):
            for index in blocks:
                self.push(self.fourth(index, 0), self.fourth(index, 3), self.side.at[plane, k], "right", 1)
                self.push(self.fourth(index, 0), self.fourth(index, 1), self.side.at[plane, k], "left", 1)
        for index in blocks:
            self.move(index, self.twin.at[0], "twin")

    def ring_step(self, k):
        blocks = self.batch(0, k)
        if k == 0:
            self.await_near(self.local.at[0], 1)
        else:
            self.await_near(self.ring.at[k - 1], len(blocks))
        if k <= 3:
            self.move(blocks[0], self.ring.at[k], "up", 0 if k == 3 else None)
            self.move(blocks[-1], self.ring.at[k], "down", 1 if k == 3 else None)
        for index in blocks:
            self.move(index, self.cross.at[k], "above", 0)
            self.move(index, self.cross.at[k], "below", 1)
        self.spread(0, k)

    def cross_step(self, k):
        self.await_near(self.cross.at[k], len(self.batch(1, k)))
        self.spread(1, k)

    def side_step(self, plane, k):
        blocks = self.batch(plane, k)
        self.await_far(self.side.at[plane, k], len(blocks), 2)
        sem = self.second.at[plane, k]
        halves = (0, 1) if len(blocks) == 1 else (None, None)
        self.push(self.fourth(blocks[0], 3, halves[0]), self.fourth(blocks[0], 2, halves[0]), sem, "right", 1)
        self.push(self.fourth(blocks[-1], 1, halves[1]), self.fourth(blocks[-1], 2, halves[1]), sem, "left", 1)

    def last_step(self, plane, k):
        blocks = self.batch(plane, k)
        if (plane, k) == (0, 0):
            self.await_far(self.local.at[1], 1, 3)
        else:
            self.await_far(self.second.at[plane, k], len(blocks), 1)
        for index in blocks:
            view = self.far.at[self.groups, index]
            self.push(view, view, self.twin.at[1], "twin", 1)

    def settle(self):
        self.await_near(self.twin.at[0], 16)
        self.await_far(self.twin.at[1], 16, 3)

    def finish(self):
        self.await_near(self.sent.at[0], 31)
        self.await_far(self.sent.at[1], 31, 3)


def stage_own(here, owns, near, far, local):
    merge, qkv, out, expand = owns
    me, x = here["lon"], here["x"]

    def put(src, dst, sem):
        pltpu.make_async_copy(src, dst, sem).start()

    for half in range(2):
        rows = pl.ds(32 * half, 32)
        put(merge.at[rows, pl.ds(0, 512)], near.at[0, me, :, pl.ds(512 * half, 512)], local.at[0, 0])
        put(out.at[:, pl.ds(512 * half, 512)], near.at[1, me, pl.ds(16 * half, 16), pl.ds(512, 512)], local.at[1, 0])
    put(qkv.at[:, pl.ds(0, 512)], near.at[1, me, :, pl.ds(0, 512)], local.at[1, 0])
    put(expand.at[:, pl.ds(0, 1024)], near.at[2, me, :, pl.ds(0, 1024)], local.at[2, 0])
    for distance in range(4):
        fourth = (x + distance) % 4
        hold, base, sem = (near, WHOLE, 0) if distance == 0 else (far, (distance - 1) * FOURTH, 1)
        for half in range(2):
            src = merge.at[pl.ds(32 * half, 32), pl.ds(pl.multiple_of(512 + 128 * fourth, 128), 128)]
            put(src, hold.at[0, me, :, pl.ds(base + 128 * half, 128)], local.at[0, sem])
        src = qkv.at[:, pl.ds(pl.multiple_of(512 + 256 * fourth, 256), 256)]
        put(src, hold.at[1, me, :, pl.ds(base, 256)], local.at[1, sem])
        src = expand.at[:, pl.ds(pl.multiple_of(1024 + 256 * fourth, 256), 256)]
        put(src, hold.at[2, me, :, pl.ds(base, 256)], local.at[2, sem])


ORDER = (
    (0, 0, 0, 0), (0, 0, 0, 1), (0, 0, 0, 2), (3, 0, 0, 0), (3, 0, 0, 1), (3, 0, 0, 2), (1, 1, 0, 0), (1, 1, 0, 1),
    (0, 0, 1, 0), (1, 1, 0, 2), (0, 0, 1, 1), (2, 1, 0, 0), (0, 0, 1, 2), (2, 1, 0, 1), (2, 0, 1, 0), (2, 1, 0, 2),
    (1, 1, 1, 0), (0, 0, 2, 0), (2, 0, 1, 1), (3, 1, 0, 0), (1, 1, 1, 1), (0, 0, 2, 1), (2, 0, 1, 2), (3, 1, 0, 1),
    (3, 0, 1, 0), (3, 1, 0, 2), (1, 1, 1, 2), (0, 0, 2, 2), (2, 1, 1, 0), (2, 0, 2, 0), (3, 0, 1, 1), (1, 1, 2, 0),
    (0, 0, 3, 0), (2, 1, 1, 1), (2, 0, 2, 1), (3, 0, 1, 2), (1, 1, 2, 1), (0, 0, 3, 1), (2, 1, 1, 2), (2, 0, 2, 2),
    (3, 1, 1, 0), (1, 1, 2, 2), (0, 0, 3, 2), (3, 0, 2, 0), (2, 1, 2, 0), (0, 0, 4, 0), (2, 0, 3, 0), (3, 1, 1, 1),
    (1, 1, 3, 0), (3, 0, 2, 1), (0, 0, 4, 1), (2, 1, 2, 1), (2, 0, 3, 1), (1, 1, 3, 1), (3, 1, 1, 2), (3, 0, 2, 2),
    (0, 0, 4, 2), (2, 1, 2, 2), (1, 1, 3, 2), (2, 0, 3, 2), (3, 1, 2, 0), (1, 1, 4, 0), (2, 0, 4, 0), (3, 0, 3, 0),
    (1, 1, 4, 1), (2, 1, 3, 0), (2, 0, 4, 1), (3, 1, 2, 1), (3, 0, 3, 1), (1, 1, 4, 2), (2, 1, 3, 1), (2, 0, 4, 2),
    (3, 1, 2, 2), (2, 1, 3, 2), (3, 0, 3, 2), (2, 1, 4, 0), (3, 0, 4, 0), (2, 1, 4, 1), (3, 1, 3, 0), (3, 0, 4, 1),
    (2, 1, 4, 2), (3, 1, 3, 1), (3, 0, 4, 2), (3, 1, 3, 2), (3, 1, 4, 0), (3, 1, 4, 1), (3, 1, 4, 2),
)


HEADS = 4
QB = 48
GROUP = 4 * 64


def one_hot(index, width):
    out = np.zeros((len(index), width), np.float32)
    rows = np.arange(len(index))[index >= 0]
    out[rows, index[index >= 0]] = 1
    return out


def orders():
    k = np.arange(QB)
    row, col, level = k // 12, k % 12 // 2, k % 2
    valid = k < 36
    quarters = np.concatenate([np.where(valid, row * 48 + (6 * j + col) * 2 + level, -1) for j in range(4)])
    slots = []
    for slot in range(4):
        r, c = 2 * row + slot % 2, 2 * col + slot // 2
        place = (r // 3 * 2 + c // 6) * QB + r % 3 * 12 + c % 6 * 2 + level
        slots.append(np.where(valid, place, -1))
    to_quarters = one_hot(quarters, 144)
    to_merged = one_hot(np.concatenate(slots), 4 * QB)
    return [jnp.asarray(m, jnp.bfloat16) for m in (to_quarters, to_quarters.T.copy(), to_merged, to_merged.T.copy())]


def dot(a, b):
    return jnp.dot(a, b, preferred_element_type=jnp.float32)


def normed(values, gain):
    center = jnp.mean(values, axis=-1, keepdims=True)
    away = values - center
    spread = jnp.mean(away * away, axis=-1, keepdims=True)
    return (away * lax.rsqrt(spread + 1e-05) * gain).astype(jnp.bfloat16)


def attend(q, k, v, bias):
    rows = q.shape[0]
    lane = lax.broadcasted_iota(jnp.int32, (1, GROUP), 1)
    of_head = [(lane >= 64 * h) & (lane < 64 * h + 64) for h in range(HEADS)]
    stacked = jnp.concatenate([jnp.where(m, q, jnp.zeros_like(q)) for m in of_head], axis=0)
    scores = lax.dot_general(stacked, k, (((1,), (1,)), ((), ())), preferred_element_type=jnp.float32)
    scores = scores + bias
    top = jnp.max(scores, axis=-1, keepdims=True)
    weights = jnp.exp(scores - top)
    total = jnp.sum(weights, axis=-1, keepdims=True)
    mixed = dot(weights.astype(jnp.bfloat16), v) / total
    out = mixed[:rows]
    for h in range(1, HEADS):
        out = jnp.where(of_head[h], mixed[h * rows : (h + 1) * rows], out)
    return out.astype(jnp.bfloat16)


def key_bias(first_hidden, second_hidden):
    lane = lax.broadcasted_iota(jnp.int32, (1, 4 * QB), 1)
    inner = lane
    for edge in (1, 2, 3):
        inner = inner - jnp.where(lane >= edge * QB, QB, 0)
    hidden = inner >= 36
    if first_hidden is not None:
        hidden = hidden | ((lane < 2 * QB) & first_hidden)
    if second_hidden is not None:
        hidden = hidden | ((lane >= 2 * QB) & second_hidden)
    return jnp.where(hidden, jnp.float32(-1e30), jnp.float32(0))


EARLY = 30


def window_span(w, n):
    return slice(max(2 * w - 1, 0), min(2 * w + 1, n))


def attend_window(here, q, kv, att, wi, wj, last, rows, groups):
    inner = q.shape[3]
    cols = window_span(wj, q.shape[1])
    bias = key_bias(
        here["north_pole"] if wi == 0 else None, here["south_pole"] if wi == last else None
    )
    for g in range(groups):
        lanes = slice(g * GROUP, g * GROUP + GROUP)
        vlanes = slice(inner + g * GROUP, inner + g * GROUP + GROUP)
        queries = q[rows, cols, :, lanes]
        out = attend(
            queries.reshape(-1, GROUP),
            kv[2 * wi : 2 * wi + 2, 2 * wj : 2 * wj + 2, :, lanes].reshape(-1, GROUP),
            kv[2 * wi : 2 * wi + 2, 2 * wj : 2 * wj + 2, :, vlanes].reshape(-1, GROUP),
            bias,
        )
        att[rows, cols, :, lanes] = out.reshape(queries.shape)


def kernel(*refs):
    (tokens, gain_down, qkv_down, out_down, merge_gain, gain_mid, gain_up, qkv_up, out_up,
     to_quarters, from_quarters, to_merged, from_merged) = refs[:13]
    owns = refs[13:17]
    result = refs[17]
    near, far = refs[18:20]
    (token_rows, x_down, kv_down, q_fine, att_fine, fine_packed, fine_landed, fine_ext, merged, x_mid,
     q_mid, kv_mid, att_mid, coarse_out, expanded, joined, kv_up) = refs[20:37]
    ring, cross, side, second, twin, sent, local, halo_send, halo_recv = refs[37:]
    here = places()
    barrier = pltpu.get_barrier_semaphore()
    greeted = [here[to] for to in ("up", "down", "above", "below", "right", "left", "twin")]
    greeted += [here[to] for to in ("north", "south", "west", "east")]
    for to in greeted:
        pl.semaphore_signal(barrier, inc=1, device_id=to, device_id_type=MESH)
    stage_own(here, owns, near, far, local)
    pl.semaphore_wait(barrier, len(greeted))
    gathers = [
        Gather(here, pl.ds(i, 1), near, far,
               *(s.at[i] for s in (ring, cross, side, second, twin, sent, local)))
        for i in range(3)
    ]
    done = [0]

    def move(steps):
        for kind, plane, k, group in ORDER[done[0] : done[0] + steps]:
            g = gathers[group]
            if kind == 0:
                g.ring_step(k)
            elif kind == 1:
                g.cross_step(k)
            elif kind == 2:
                g.side_step(plane, k)
            else:
                g.last_step(plane, k)
        done[0] += steps

    copies = []

    def copy(src, dst, to):
        index = len(copies)
        copies.append(pltpu.make_async_remote_copy(
            src_ref=src, dst_ref=dst, send_sem=halo_send.at[index], recv_sem=halo_recv.at[index],
            device_id=here[to], device_id_type=MESH,
        ))
        return copies[-1]

    def columns(kv, rows):
        n = kv.shape[1] - 2
        return [
            copy(kv.at[rows, pl.ds(1, 1)], kv.at[rows, pl.ds(n + 1, 1)], "west"),
            copy(kv.at[rows, pl.ds(n, 1)], kv.at[rows, pl.ds(0, 1)], "east"),
        ]

    def start(group):
        for c in group:
            c.start()

    def wait(group):
        for c in group:
            c.wait_recv()

    token_halo = [
        copy(tokens.at[pl.ds(0, 144)], token_rows.at[1], "north"),
        copy(tokens.at[pl.ds(432, 144)], token_rows.at[0], "south"),
    ]
    down_sides = columns(kv_down, pl.ds(1, 4))
    down_corners = columns(kv_down, pl.ds(0, 1)) + columns(kv_down, pl.ds(5, 1))
    fine_halo = [
        copy(fine_packed.at[i], fine_landed.at[(i + 2) % 4], "north" if i < 2 else "south") for i in range(4)
    ]
    mid_sides = columns(kv_mid, pl.ds(0, 4))
    up_sides = columns(kv_up, pl.ds(0, 6))
    bf16 = jnp.bfloat16

    def down_project(row, source):
        x = dot(to_quarters[...], source)
        n = normed(x, gain_down[...])
        if 0 < row < 5:
            x_down[row - 1] = x.astype(bf16)
            out = dot(n, qkv_down[...])
            q_fine[row - 1] = (out[:, :256] * 0.125).astype(bf16).reshape(4, QB, 256)
            out = out[:, 256:]
        else:
            out = dot(n, qkv_down[:, 256:])
        kv_down[row, 1:5] = out.astype(bf16).reshape(4, QB, 512)

    def down_output(i):
        branch = dot(att_fine[i].reshape(192, 256), out_down[...])
        out = (x_down[i].astype(jnp.float32) + branch).astype(bf16)
        fine_ext[2 + i] = out.reshape(4, QB, 512)
        fine_packed[i] = dot(from_quarters[...], out).astype(bf16)
        fine_halo[i].start()

    def fine_window(kv, wi, wj):
        attend_window(here, q_fine, kv, att_fine, wi, wj, 2, window_span(wi, 4), 1)

    def merge_rows(i):
        for j in range(2):
            quad = fine_ext[2 * i : 2 * i + 2, 2 * j : 2 * j + 2].reshape(192, 512)
            spots = dot(to_merged[...], quad)
            parts = [spots[QB * k : QB * k + QB] for k in range(4)]
            center = sum(jnp.sum(p, axis=-1, keepdims=True) for p in parts) * (1 / 2048)
            parts = [p - center for p in parts]
            spread = sum(jnp.sum(p * p, axis=-1, keepdims=True) for p in parts) * (1 / 2048)
            factor = lax.rsqrt(spread + 1e-05)
            for k in range(4):
                lanes = slice(512 * k, 512 * k + 512)
                merged[2 * i + j, :, lanes] = (parts[k] * factor * merge_gain[:, lanes]).astype(bf16)

    start(token_halo)
    move(1)
    for i in range(4):
        down_project(i + 1, tokens[144 * i : 144 * i + 144])
    start(down_sides)
    move(5)
    fine_window(kv_down, 1, 1)
    wait(down_sides)
    fine_window(kv_down, 1, 0)
    fine_window(kv_down, 1, 2)
    down_output(1)
    down_output(2)
    wait(token_halo)
    down_project(0, token_rows[0])
    down_project(5, token_rows[1])
    start(down_corners)
    move(2)
    for wi in (0, 2):
        fine_window(kv_down, wi, 1)
        move(1)
    wait(down_corners)
    for wi, wj in ((0, 0), (0, 2), (2, 0), (2, 2)):
        fine_window(kv_down, wi, wj)
    down_output(0)
    down_output(3)
    move(EARLY)
    merge_rows(1)
    merge_rows(2)
    move(len(ORDER))
    wait(fine_halo)
    for i, row in enumerate((0, 1, 6, 7)):
        fine_ext[row] = dot(to_quarters[...], fine_landed[i]).astype(bf16).reshape(4, QB, 512)
    merge_rows(0)
    merge_rows(3)
    fourths = [(here["x"] + d) % 4 for d in range(4)]

    def held(group, d):
        return near[group, :, :, WHOLE:] if d == 0 else far[group, :, :, 256 * (d - 1) : 256 * d]

    gathers[0].settle()
    n_merged = merged[...].reshape(384, 2048)
    weight = jnp.stack([near[0, :, :, :512], near[0, :, :, 512:1024]], axis=1).reshape(2048, 512)
    x_mid[:, :512] = dot(n_merged, weight).astype(bf16)
    for d in range(4):
        hold = held(0, d)
        weight = jnp.stack([hold[:, :, :128], hold[:, :, 128:]], axis=1).reshape(2048, 128)
        lanes = pl.ds(pl.multiple_of(512 + 128 * fourths[d], 128), 128)
        x_mid[:, lanes] = dot(n_merged, weight).astype(bf16)
    n_mid = normed(x_mid[...].astype(jnp.float32), gain_mid[...])
    gathers[1].settle()
    for d in range(4):
        out = dot(n_mid, held(1, d).reshape(1024, 256))
        lanes = pl.ds(pl.multiple_of(256 * fourths[d], 256), 256)
        kv_mid[:, 1:3, :, lanes] = out.astype(bf16).reshape(4, 2, QB, 256)
    start(mid_sides)
    out = dot(n_mid, near[1, :, :, :512].reshape(1024, 512)) * 0.125
    q_mid[...] = out.astype(bf16).reshape(4, 2, QB, 512)
    wait(mid_sides)
    for wi in range(2):
        for wj in range(2):
            attend_window(here, q_mid, kv_mid, att_mid, wi, wj, 1, slice(2 * wi, 2 * wi + 2), 2)
    for c in range(2):
        lanes = slice(512 * c, 512 * c + 512)
        weight = near[1, :, 16 * c : 16 * c + 16, 512:1024].reshape(512, 512)
        out = dot(att_mid[...].reshape(384, 512), weight)
        coarse_out[:, lanes] = (x_mid[:, lanes].astype(jnp.float32) + out).astype(bf16)
    gathers[2].settle()
    for k in range(2):
        out = dot(coarse_out[...], near[2, :, :, 512 * k : 512 * k + 512].reshape(1024, 512))
        expanded[:, k] = out.astype(bf16).reshape(8, QB, 512)
    for d in range(4):
        out = dot(coarse_out[...], held(2, d).reshape(1024, 256))
        lanes = pl.ds(pl.multiple_of(256 * (fourths[d] % 2), 256), 256)
        expanded[:, 2 + fourths[d] // 2, :, lanes] = out.astype(bf16).reshape(8, QB, 256)
    for row in range(1, 7):
        half = row % 2
        pick = from_merged[96 * half : 96 * half + 96]
        pieces = []
        for j in range(2):
            grown = dot(pick, expanded[2 * (row // 2) + j].reshape(192, 512))
            pieces.append(grown + fine_ext[row, 2 * j : 2 * j + 2].reshape(96, 512).astype(jnp.float32))
        x = jnp.concatenate(pieces, axis=0).astype(bf16)
        n = normed(x.astype(jnp.float32), gain_up[...])
        if 1 < row < 6:
            joined[row - 2] = x
            out = dot(n, qkv_up[...])
            q_fine[row - 2] = (out[:, :256] * 0.125).astype(bf16).reshape(4, QB, 256)
            out = out[:, 256:]
        else:
            out = dot(n, qkv_up[:, 256:])
        kv_up[row - 1, 1:5] = out.astype(bf16).reshape(4, QB, 512)
    start(up_sides)
    for wi in range(3):
        fine_window(kv_up, wi, 1)
    wait(up_sides)
    for wi in range(3):
        fine_window(kv_up, wi, 0)
        fine_window(kv_up, wi, 2)
    for i in range(4):
        branch = dot(att_fine[i].reshape(192, 256), out_up[...])
        out = (joined[i].astype(jnp.float32) + branch).astype(bf16)
        result[144 * i : 144 * i + 144] = dot(from_quarters[...], out).astype(bf16)
    for g in gathers:
        g.finish()
    for c in copies:
        c.wait_send()


def on_device(tokens, gain_down, qkv_down, out_down, merge_gain, merge_weight, gain_mid, qkv_mid,
              out_mid, expand_weight, gain_up, qkv_up, out_up):
    weights = (merge_weight, qkv_mid, out_mid, expand_weight)
    row = lambda g: g.reshape(1, -1)
    bf16 = jnp.bfloat16
    vmem = pl.BlockSpec(memory_space=pltpu.VMEM)
    out = pl.pallas_call(
        kernel,
        out_shape=jax.ShapeDtypeStruct((576, 512), bf16),
        in_specs=[vmem] * 13 + [pl.BlockSpec(memory_space=pl.ANY)] * 4,
        out_specs=vmem,
        scratch_shapes=[
            pltpu.VMEM((3, 32, 32, WHOLE + FOURTH), bf16),
            pltpu.VMEM((3, 32, 32, 3 * FOURTH), bf16),
            pltpu.VMEM((2, 144, 512), bf16),
            pltpu.VMEM((4, 192, 512), bf16),
            pltpu.VMEM((6, 6, QB, 512), bf16),
            pltpu.VMEM((4, 4, QB, 256), bf16),
            pltpu.VMEM((4, 4, QB, 256), bf16),
            pltpu.VMEM((4, 144, 512), bf16),
            pltpu.VMEM((4, 144, 512), bf16),
            pltpu.VMEM((8, 4, QB, 512), bf16),
            pltpu.VMEM((8, QB, 2048), bf16),
            pltpu.VMEM((384, 1024), bf16),
            pltpu.VMEM((4, 2, QB, 512), bf16),
            pltpu.VMEM((4, 4, QB, 1024), bf16),
            pltpu.VMEM((4, 2, QB, 512), bf16),
            pltpu.VMEM((384, 1024), bf16),
            pltpu.VMEM((8, 4, QB, 512), bf16),
            pltpu.VMEM((4, 192, 512), bf16),
            pltpu.VMEM((6, 6, QB, 512), bf16),
            pltpu.SemaphoreType.DMA((3, 4)),
            pltpu.SemaphoreType.DMA((3, 5)),
            pltpu.SemaphoreType.DMA((3, 2, 5)),
            pltpu.SemaphoreType.DMA((3, 2, 5)),
            pltpu.SemaphoreType.DMA((3, 2)),
            pltpu.SemaphoreType.DMA((3, 2)),
            pltpu.SemaphoreType.DMA((3, 2)),
            pltpu.SemaphoreType.DMA((16,)),
            pltpu.SemaphoreType.DMA((16,)),
        ],
        compiler_params=pltpu.CompilerParams(
            collective_id=0, has_side_effects=True, vmem_limit_bytes=56 * 2**20
        ),
    )(tokens.reshape(576, 512), row(gain_down), qkv_down, out_down, row(merge_gain), row(gain_mid),
      row(gain_up), qkv_up, out_up, *orders(), *weights)
    return out.reshape(tokens.shape)


def solution(mesh):
    return jax.shard_map(
        on_device,
        mesh=mesh,
        in_specs=(
            P("lat", "lon", None, None), P(), P(), P(), P(), P("lon", None), P(), P("lon", None),
            P("lon", None), P("lon", None), P(), P(), P(),
        ),
        out_specs=P("lat", "lon", None, None),
        check_vma=False,
    )
```

```python
import jax
import jax.numpy as jnp
import numpy as np
from jax import lax
from jax.experimental import pallas as pl
from jax.experimental.pallas import tpu as pltpu
from jax.sharding import PartitionSpec as P

MESH = pl.DeviceIdType.MESH


def places():
    lat, lon = lax.axis_index("lat"), lax.axis_index("lon")
    lats = lax.axis_size("lat")
    core = lon % 2
    y = (lon // 2) % 8
    plane = lon // 16
    x = lat % 4
    at = lambda p, yy: p * 16 + ((yy + 16) % 8) * 2 + core
    return dict(
        north_pole=lat == 0, south_pole=lat == lats - 1,
        north=((lat + lats - 1) % lats, lon), south=((lat + 1) % lats, lon),
        beyond=((lat + 4) % lats, lon), behind=((lat + lats - 4) % lats, lon),
        west=(lat, (lon + 31) % 32), east=(lat, (lon + 1) % 32),
        lat=lat, lon=lon, core=core, x=x, y=y, plane=plane, at=at,
        up=(lat, at(plane, y + 1)),
        down=(lat, at(plane, y - 1)),
        above=((lat + 4 * plane) % lats, at(1 - plane, y)),
        below=((lat + 4 * plane + lats - 4) % lats, at(1 - plane, y)),
        right=(lat - x + (x + 1) % 4, lon),
        left=(lat - x + (x + 3) % 4, lon),
        twin=(lat, lon + 1 - 2 * core),
    )


WHOLE, FOURTH = 1024, 256


class Gather:
    def __init__(self, here, groups, near, far, ring, cross, side, second, twin, sent, local):
        self.here, self.groups, self.near, self.far = here, groups, near, far
        self.ring, self.cross, self.side, self.second = ring, cross, side, second
        self.twin, self.sent, self.local = twin, sent, local

    def push(self, src, dst, sem, to, kind=0):
        pltpu.make_async_remote_copy(
            src_ref=src, dst_ref=dst, send_sem=self.sent.at[kind], recv_sem=sem,
            device_id=self.here[to], device_id_type=MESH,
        ).start()

    def await_near(self, sem, count):
        view = self.near.at[self.groups, pl.ds(0, count)]
        pltpu.make_async_copy(view, view, sem).wait()

    def await_far(self, sem, count, fourths):
        view = self.far.at[self.groups, pl.ds(0, count), :, pl.ds(0, fourths * FOURTH)]
        pltpu.make_async_copy(view, view, sem).wait()

    def block(self, index, half=None):
        rows = slice(None) if half is None else pl.ds(16 * half, 16)
        return self.near.at[self.groups, index, rows]

    def fourth(self, index, distance, half=None):
        rows = slice(None) if half is None else pl.ds(16 * half, 16)
        if distance == 0:
            return self.near.at[self.groups, index, rows, pl.ds(WHOLE, FOURTH)]
        return self.far.at[self.groups, index, rows, pl.ds((distance - 1) * FOURTH, FOURTH)]

    def move(self, index, sem, to, half=None):
        self.push(self.block(index, half), self.block(index, half), sem, to)

    def batch(self, plane, k):
        at, y = self.here["at"], self.here["y"]
        p = self.here["plane"] if plane == 0 else 1 - self.here["plane"]
        return [at(p, y + k)] if k in (0, 4) else [at(p, y - k), at(p, y + k)]

    def spread(self, plane, k):
        blocks = self.batch(plane, k)
        if (plane, k) != (0, 0):
            for index in blocks:
                self.push(self.fourth(index, 0), self.fourth(index, 3), self.side.at[plane, k], "right", 1)
                self.push(self.fourth(index, 0), self.fourth(index, 1), self.side.at[plane, k], "left", 1)
        for index in blocks:
            self.move(index, self.twin.at[0], "twin")

    def ring_step(self, k):
        blocks = self.batch(0, k)
        if k == 0:
            self.await_near(self.local.at[0], 1)
        else:
            self.await_near(self.ring.at[k - 1], len(blocks))
        if k <= 3:
            self.move(blocks[0], self.ring.at[k], "up", 0 if k == 3 else None)
            self.move(blocks[-1], self.ring.at[k], "down", 1 if k == 3 else None)
        for index in blocks:
            self.move(index, self.cross.at[k], "above", 0)
            self.move(index, self.cross.at[k], "below", 1)
        self.spread(0, k)

    def cross_step(self, k):
        self.await_near(self.cross.at[k], len(self.batch(1, k)))
        self.spread(1, k)

    def side_step(self, plane, k):
        blocks = self.batch(plane, k)
        self.await_far(self.side.at[plane, k], len(blocks), 2)
        sem = self.second.at[plane, k]
        halves = (0, 1) if len(blocks) == 1 else (None, None)
        self.push(self.fourth(blocks[0], 3, halves[0]), self.fourth(blocks[0], 2, halves[0]), sem, "right", 1)
        self.push(self.fourth(blocks[-1], 1, halves[1]), self.fourth(blocks[-1], 2, halves[1]), sem, "left", 1)

    def last_step(self, plane, k):
        blocks = self.batch(plane, k)
        if (plane, k) == (0, 0):
            self.await_far(self.local.at[1], 1, 3)
        else:
            self.await_far(self.second.at[plane, k], len(blocks), 1)
        for index in blocks:
            view = self.far.at[self.groups, index]
            self.push(view, view, self.twin.at[1], "twin", 1)

    def settle(self):
        self.await_near(self.twin.at[0], 16)
        self.await_far(self.twin.at[1], 16, 3)

    def finish(self):
        self.await_near(self.sent.at[0], 31)
        self.await_far(self.sent.at[1], 31, 3)


def stage_own(here, owns, near, far, local):
    merge, qkv, out, expand = owns
    me, x = here["lon"], here["x"]

    def put(src, dst, sem):
        pltpu.make_async_copy(src, dst, sem).start()

    for half in range(2):
        rows = pl.ds(32 * half, 32)
        put(merge.at[rows, pl.ds(0, 512)], near.at[0, me, :, pl.ds(512 * half, 512)], local.at[0, 0])
        put(out.at[:, pl.ds(512 * half, 512)], near.at[1, me, pl.ds(16 * half, 16), pl.ds(512, 512)], local.at[1, 0])
    put(qkv.at[:, pl.ds(0, 512)], near.at[1, me, :, pl.ds(0, 512)], local.at[1, 0])
    put(expand.at[:, pl.ds(0, 1024)], near.at[2, me, :, pl.ds(0, 1024)], local.at[2, 0])
    for distance in range(4):
        fourth = (x + distance) % 4
        hold, base, sem = (near, WHOLE, 0) if distance == 0 else (far, (distance - 1) * FOURTH, 1)
        for half in range(2):
            src = merge.at[pl.ds(32 * half, 32), pl.ds(pl.multiple_of(512 + 128 * fourth, 128), 128)]
            put(src, hold.at[0, me, :, pl.ds(base + 128 * half, 128)], local.at[0, sem])
        src = qkv.at[:, pl.ds(pl.multiple_of(512 + 256 * fourth, 256), 256)]
        put(src, hold.at[1, me, :, pl.ds(base, 256)], local.at[1, sem])
        src = expand.at[:, pl.ds(pl.multiple_of(1024 + 256 * fourth, 256), 256)]
        put(src, hold.at[2, me, :, pl.ds(base, 256)], local.at[2, sem])


ORDER = (
    (0, 0, 0, 0), (0, 0, 0, 1), (0, 0, 0, 2), (3, 0, 0, 0), (3, 0, 0, 1), (3, 0, 0, 2), (1, 1, 0, 0), (1, 1, 0, 1),
    (0, 0, 1, 0), (1, 1, 0, 2), (0, 0, 1, 1), (2, 1, 0, 0), (0, 0, 1, 2), (2, 1, 0, 1), (2, 0, 1, 0), (2, 1, 0, 2),
    (1, 1, 1, 0), (0, 0, 2, 0), (2, 0, 1, 1), (3, 1, 0, 0), (1, 1, 1, 1), (0, 0, 2, 1), (2, 0, 1, 2), (3, 1, 0, 1),
    (3, 0, 1, 0), (3, 1, 0, 2), (1, 1, 1, 2), (0, 0, 2, 2), (2, 1, 1, 0), (2, 0, 2, 0), (3, 0, 1, 1), (1, 1, 2, 0),
    (0, 0, 3, 0), (2, 1, 1, 1), (2, 0, 2, 1), (3, 0, 1, 2), (1, 1, 2, 1), (0, 0, 3, 1), (2, 1, 1, 2), (2, 0, 2, 2),
    (3, 1, 1, 0), (1, 1, 2, 2), (0, 0, 3, 2), (3, 0, 2, 0), (2, 1, 2, 0), (0, 0, 4, 0), (2, 0, 3, 0), (3, 1, 1, 1),
    (1, 1, 3, 0), (3, 0, 2, 1), (0, 0, 4, 1), (2, 1, 2, 1), (2, 0, 3, 1), (1, 1, 3, 1), (3, 1, 1, 2), (3, 0, 2, 2),
    (0, 0, 4, 2), (2, 1, 2, 2), (1, 1, 3, 2), (2, 0, 3, 2), (3, 1, 2, 0), (1, 1, 4, 0), (2, 0, 4, 0), (3, 0, 3, 0),
    (1, 1, 4, 1), (2, 1, 3, 0), (2, 0, 4, 1), (3, 1, 2, 1), (3, 0, 3, 1), (1, 1, 4, 2), (2, 1, 3, 1), (2, 0, 4, 2),
    (3, 1, 2, 2), (2, 1, 3, 2), (3, 0, 3, 2), (2, 1, 4, 0), (3, 0, 4, 0), (2, 1, 4, 1), (3, 1, 3, 0), (3, 0, 4, 1),
    (2, 1, 4, 2), (3, 1, 3, 1), (3, 0, 4, 2), (3, 1, 3, 2), (3, 1, 4, 0), (3, 1, 4, 1), (3, 1, 4, 2),
)


HEADS = 4
QB = 48
GROUP = 4 * 64


def one_hot(index, width):
    out = np.zeros((len(index), width), np.float32)
    rows = np.arange(len(index))[index >= 0]
    out[rows, index[index >= 0]] = 1
    return out


def orders():
    k = np.arange(QB)
    row, col, level = k // 12, k % 12 // 2, k % 2
    valid = k < 36
    quarters = np.concatenate([np.where(valid, row * 48 + (6 * j + col) * 2 + level, -1) for j in range(4)])
    slots = []
    for slot in range(4):
        r, c = 2 * row + slot % 2, 2 * col + slot // 2
        place = (r // 3 * 2 + c // 6) * QB + r % 3 * 12 + c % 6 * 2 + level
        slots.append(np.where(valid, place, -1))
    to_quarters = one_hot(quarters, 144)
    to_merged = one_hot(np.concatenate(slots), 4 * QB)
    return [jnp.asarray(m, jnp.bfloat16) for m in (to_quarters, to_quarters.T.copy(), to_merged, to_merged.T.copy())]


def dot(a, b):
    return jnp.dot(a, b, preferred_element_type=jnp.float32)


def normed(values, gain):
    center = jnp.mean(values, axis=-1, keepdims=True)
    away = values - center
    spread = jnp.mean(away * away, axis=-1, keepdims=True)
    return (away * lax.rsqrt(spread + 1e-05) * gain).astype(jnp.bfloat16)


def attend(q, k, v, bias):
    rows = q.shape[0]
    lane = lax.broadcasted_iota(jnp.int32, (1, GROUP), 1)
    of_head = [(lane >= 64 * h) & (lane < 64 * h + 64) for h in range(HEADS)]
    stacked = jnp.concatenate([jnp.where(m, q, jnp.zeros_like(q)) for m in of_head], axis=0)
    scores = lax.dot_general(stacked, k, (((1,), (1,)), ((), ())), preferred_element_type=jnp.float32)
    scores = scores + bias
    top = jnp.max(scores, axis=-1, keepdims=True)
    weights = jnp.exp(scores - top)
    total = jnp.sum(weights, axis=-1, keepdims=True)
    mixed = dot(weights.astype(jnp.bfloat16), v) / total
    out = mixed[:rows]
    for h in range(1, HEADS):
        out = jnp.where(of_head[h], mixed[h * rows : (h + 1) * rows], out)
    return out.astype(jnp.bfloat16)


def key_bias(first_hidden, second_hidden):
    lane = lax.broadcasted_iota(jnp.int32, (1, 4 * QB), 1)
    inner = lane
    for edge in (1, 2, 3):
        inner = inner - jnp.where(lane >= edge * QB, QB, 0)
    hidden = inner >= 36
    if first_hidden is not None:
        hidden = hidden | ((lane < 2 * QB) & first_hidden)
    if second_hidden is not None:
        hidden = hidden | ((lane >= 2 * QB) & second_hidden)
    return jnp.where(hidden, jnp.float32(-1e30), jnp.float32(0))


RELAY = 30
PAUSES = (6, 9, 15, 25, 36, 48, 64)


def window_span(w, n):
    return slice(max(2 * w - 1, 0), min(2 * w + 1, n))


def attend_window(here, q, kv, att, wi, wj, rows, groups, first, last):
    inner = q.shape[3]
    cols = window_span(wj, q.shape[1])
    bias = key_bias(here["north_pole"] if first else None, here["south_pole"] if last else None)
    for g in range(groups):
        lanes = slice(g * GROUP, g * GROUP + GROUP)
        vlanes = slice(inner + g * GROUP, inner + g * GROUP + GROUP)
        queries = q[rows, cols, :, lanes]
        out = attend(
            queries.reshape(-1, GROUP),
            kv[2 * wi : 2 * wi + 2, 2 * wj : 2 * wj + 2, :, lanes].reshape(-1, GROUP),
            kv[2 * wi : 2 * wi + 2, 2 * wj : 2 * wj + 2, :, vlanes].reshape(-1, GROUP),
            bias,
        )
        att[rows, cols, :, lanes] = out.reshape(queries.shape)


def kernel(*refs):
    (tokens, gain_down, qkv_down, out_down, merge_gain, gain_mid, gain_up, qkv_up, out_up,
     to_quarters, from_quarters, to_merged, from_merged) = refs[:13]
    owns = refs[13:17]
    result = refs[17]
    near, far = refs[18:20]
    (token_rows, x_down, kv_down, q_down, att_down, q_fine, att_fine, fine_ext, merged, x_mid,
     q_mid, kv_mid, att_mid, coarse_out, expanded, joined, kv_up) = refs[20:37]
    ring, cross, side, second, twin, sent, local, halo_send, halo_recv = refs[37:]
    here = places()
    barrier = pltpu.get_barrier_semaphore()
    greeted = [here[to] for to in ("up", "down", "above", "below", "right", "left", "twin")]
    greeted += [here[to] for to in ("north", "south", "west", "east", "beyond", "behind")]
    for to in greeted:
        pl.semaphore_signal(barrier, inc=1, device_id=to, device_id_type=MESH)
    stage_own(here, owns, near, far, local)
    pl.semaphore_wait(barrier, len(greeted))
    gathers = [
        Gather(here, pl.ds(i, 1), near, far,
               *(s.at[i] for s in (ring, cross, side, second, twin, sent, local)))
        for i in range(3)
    ]
    done = [0]

    def move(until):
        for kind, plane, k, group in ORDER[done[0] : until]:
            g = gathers[group]
            if kind == 0:
                g.ring_step(k)
            elif kind == 1:
                g.cross_step(k)
            elif kind == 2:
                g.side_step(plane, k)
            else:
                g.last_step(plane, k)
        done[0] = max(done[0], until)

    copies = []

    def copy(src, dst, to):
        index = len(copies)
        copies.append(pltpu.make_async_remote_copy(
            src_ref=src, dst_ref=dst, send_sem=halo_send.at[index], recv_sem=halo_recv.at[index],
            device_id=here[to], device_id_type=MESH,
        ))
        return copies[-1]

    def columns(kv, rows):
        n = kv.shape[1] - 2
        return [
            copy(kv.at[rows, pl.ds(1, 1)], kv.at[rows, pl.ds(n + 1, 1)], "west"),
            copy(kv.at[rows, pl.ds(n, 1)], kv.at[rows, pl.ds(0, 1)], "east"),
        ]

    def start(group):
        for c in group:
            c.start()

    def wait(group):
        for c in group:
            c.wait_recv()

    def token_copies(near_by):
        both = []
        for chunk, slot, to, edge, turn in (
            (near_by, 3 + near_by, "north", 0, "left"), (3 - near_by, 2 - near_by, "south", 3, "right")
        ):
            detour = (here["x"] == edge) & (here["core"] == 1)
            index = len(copies)
            copies.append(pltpu.make_async_remote_copy(
                src_ref=tokens.at[pl.ds(144 * chunk, 144)],
                dst_ref=token_rows.at[jnp.where(detour, 6 + near_by, slot)],
                send_sem=halo_send.at[index],
                recv_sem=halo_recv.at[jnp.where(detour, RELAY + near_by, index)],
                device_id=(jnp.where(detour, here[turn][0], here[to][0]), here["lon"]),
                device_id_type=MESH,
            ))
            both.append(copies[-1])
        return both

    def relay(i, begin):
        for edge, slot, index, to in ((0, 2 - i, 2 * i + 1, "beyond"), (3, 3 + i, 2 * i, "behind")):
            @pl.when((here["x"] == edge) & (here["core"] == 1))
            def _():
                c = pltpu.make_async_remote_copy(
                    src_ref=token_rows.at[6 + i], dst_ref=token_rows.at[slot],
                    send_sem=halo_send.at[RELAY + i], recv_sem=halo_recv.at[index],
                    device_id=here[to], device_id_type=MESH,
                )
                if begin:
                    view = token_rows.at[6 + i]
                    pltpu.make_async_copy(view, view, halo_recv.at[RELAY + i]).wait()
                    c.start()
                else:
                    c.wait_send()

    token_halo = [token_copies(i) for i in range(3)]
    down_sides = columns(kv_down, pl.ds(3, 4))
    down_corners = [columns(kv_down, pl.ds(2 - i, 1)) + columns(kv_down, pl.ds(7 + i, 1)) for i in range(3)]
    mid_sides = [columns(kv_mid, pl.ds(2 * i, 2)) for i in range(2)]
    up_sides = [columns(kv_up, pl.ds(2 * i, 2)) for i in range(3)]
    bf16 = jnp.bfloat16

    def down_project(row, source):
        x = dot(to_quarters[...], source)
        n = normed(x, gain_down[...])
        if 0 < row < 9:
            x_down[row - 1] = x.astype(bf16)
            out = dot(n, qkv_down[...])
            q_down[row - 1] = (out[:, :256] * 0.125).astype(bf16).reshape(4, QB, 256)
            out = out[:, 256:]
        else:
            out = dot(n, qkv_down[:, 256:])
        kv_down[row, 1:5] = out.astype(bf16).reshape(4, QB, 512)

    def down_borders(i):
        for slot, index in ((3 + i, 2 * i), (2 - i, 2 * i + 1)):
            view = token_rows.at[slot]
            pltpu.make_async_copy(view, view, halo_recv.at[index]).wait()
        down_project(2 - i, token_rows[2 - i])
        down_project(7 + i, token_rows[3 + i])
        start(down_corners[i])

    def down_window(wi):
        for wj in (1, 0, 2):
            attend_window(here, q_down, kv_down, att_down, wi, wj, window_span(wi, 8), 1, wi == 1, wi == 3)

    def down_output(i):
        branch = dot(att_down[i].reshape(192, 256), out_down[...])
        fine_ext[i] = (x_down[i].astype(jnp.float32) + branch).astype(bf16).reshape(4, QB, 512)

    def fine_window(kv, wi, wj):
        attend_window(here, q_fine, kv, att_fine, wi, wj, window_span(wi, 4), 1, wi == 0, wi == 2)

    def merge_rows(i):
        for j in range(2):
            quad = fine_ext[2 * i : 2 * i + 2, 2 * j : 2 * j + 2].reshape(192, 512)
            spots = dot(to_merged[...], quad)
            parts = [spots[QB * k : QB * k + QB] for k in range(4)]
            center = sum(jnp.sum(p, axis=-1, keepdims=True) for p in parts) * (1 / 2048)
            parts = [p - center for p in parts]
            spread = sum(jnp.sum(p * p, axis=-1, keepdims=True) for p in parts) * (1 / 2048)
            factor = lax.rsqrt(spread + 1e-05)
            for k in range(4):
                lanes = slice(512 * k, 512 * k + 512)
                merged[2 * i + j, :, lanes] = (parts[k] * factor * merge_gain[:, lanes]).astype(bf16)

    start(token_halo[0])
    move(1)
    for i in range(4):
        down_project(i + 3, tokens[144 * i : 144 * i + 144])
    start(down_sides)
    start(token_halo[1])
    move(PAUSES[0])
    start(token_halo[2])
    relay(0, True)
    move(PAUSES[1])
    wait(down_sides)
    down_window(2)
    relay(1, True)
    move(PAUSES[2])
    down_borders(0)
    relay(2, True)
    move(PAUSES[3])
    wait(down_corners[0])
    down_window(1)
    down_window(3)
    for i in range(1, 7):
        down_output(i)
    move(PAUSES[4])
    down_borders(1)
    merge_rows(1)
    merge_rows(2)
    move(PAUSES[5])
    down_borders(2)
    move(PAUSES[6])
    wait(down_corners[1])
    wait(down_corners[2])
    down_window(0)
    down_window(4)
    down_output(0)
    down_output(7)
    merge_rows(0)
    merge_rows(3)
    move(len(ORDER))
    fourths = [(here["x"] + d) % 4 for d in range(4)]

    def held(group, d):
        return near[group, :, :, WHOLE:] if d == 0 else far[group, :, :, 256 * (d - 1) : 256 * d]

    gathers[0].settle()
    n_merged = merged[...].reshape(384, 2048)
    weight = jnp.stack([near[0, :, :, :512], near[0, :, :, 512:1024]], axis=1).reshape(2048, 512)
    x_mid[:, :512] = dot(n_merged, weight).astype(bf16)
    for d in range(4):
        hold = held(0, d)
        weight = jnp.stack([hold[:, :, :128], hold[:, :, 128:]], axis=1).reshape(2048, 128)
        lanes = pl.ds(pl.multiple_of(512 + 128 * fourths[d], 128), 128)
        x_mid[:, lanes] = dot(n_merged, weight).astype(bf16)
    n_mid = normed(x_mid[...].astype(jnp.float32), gain_mid[...])
    gathers[1].settle()
    for half in range(2):
        for d in range(4):
            out = dot(n_mid[192 * half : 192 * half + 192], held(1, d).reshape(1024, 256))
            lanes = pl.ds(pl.multiple_of(256 * fourths[d], 256), 256)
            kv_mid[2 * half : 2 * half + 2, 1:3, :, lanes] = out.astype(bf16).reshape(2, 2, QB, 256)
        start(mid_sides[half])
    out = dot(n_mid, near[1, :, :, :512].reshape(1024, 512)) * 0.125
    q_mid[...] = out.astype(bf16).reshape(4, 2, QB, 512)
    for wi in range(2):
        wait(mid_sides[wi])
        for wj in range(2):
            attend_window(here, q_mid, kv_mid, att_mid, wi, wj, slice(2 * wi, 2 * wi + 2), 2, wi == 0, wi == 1)
    for c in range(2):
        lanes = slice(512 * c, 512 * c + 512)
        weight = near[1, :, 16 * c : 16 * c + 16, 512:1024].reshape(512, 512)
        out = dot(att_mid[...].reshape(384, 512), weight)
        coarse_out[:, lanes] = (x_mid[:, lanes].astype(jnp.float32) + out).astype(bf16)
    gathers[2].settle()
    for k in range(2):
        out = dot(coarse_out[...], near[2, :, :, 512 * k : 512 * k + 512].reshape(1024, 512))
        expanded[:, k] = out.astype(bf16).reshape(8, QB, 512)
    for d in range(4):
        out = dot(coarse_out[...], held(2, d).reshape(1024, 256))
        lanes = pl.ds(pl.multiple_of(256 * (fourths[d] % 2), 256), 256)
        expanded[:, 2 + fourths[d] // 2, :, lanes] = out.astype(bf16).reshape(8, QB, 256)
    for row in range(1, 7):
        half = row % 2
        pick = from_merged[96 * half : 96 * half + 96]
        pieces = []
        for j in range(2):
            grown = dot(pick, expanded[2 * (row // 2) + j].reshape(192, 512))
            pieces.append(grown + fine_ext[row, 2 * j : 2 * j + 2].reshape(96, 512).astype(jnp.float32))
        x = jnp.concatenate(pieces, axis=0).astype(bf16)
        n = normed(x.astype(jnp.float32), gain_up[...])
        if 1 < row < 6:
            joined[row - 2] = x
            out = dot(n, qkv_up[...])
            q_fine[row - 2] = (out[:, :256] * 0.125).astype(bf16).reshape(4, QB, 256)
            out = out[:, 256:]
        else:
            out = dot(n, qkv_up[:, 256:])
        kv_up[row - 1, 1:5] = out.astype(bf16).reshape(4, QB, 512)
        if row % 2 == 0:
            start(up_sides[row // 2 - 1])
    for wi in range(3):
        fine_window(kv_up, wi, 1)
    for wi in range(3):
        wait(up_sides[wi])
        fine_window(kv_up, wi, 0)
        fine_window(kv_up, wi, 2)
    for i in range(4):
        branch = dot(att_fine[i].reshape(192, 256), out_up[...])
        out = (joined[i].astype(jnp.float32) + branch).astype(bf16)
        result[144 * i : 144 * i + 144] = dot(from_quarters[...], out).astype(bf16)
    for g in gathers:
        g.finish()
    for c in copies:
        c.wait_send()
    for i in range(3):
        relay(i, False)


def on_device(tokens, gain_down, qkv_down, out_down, merge_gain, merge_weight, gain_mid, qkv_mid,
              out_mid, expand_weight, gain_up, qkv_up, out_up):
    weights = (merge_weight, qkv_mid, out_mid, expand_weight)
    row = lambda g: g.reshape(1, -1)
    bf16 = jnp.bfloat16
    vmem = pl.BlockSpec(memory_space=pltpu.VMEM)
    out = pl.pallas_call(
        kernel,
        out_shape=jax.ShapeDtypeStruct((576, 512), bf16),
        in_specs=[vmem] * 13 + [pl.BlockSpec(memory_space=pl.ANY)] * 4,
        out_specs=vmem,
        scratch_shapes=[
            pltpu.VMEM((3, 32, 32, WHOLE + FOURTH), bf16),
            pltpu.VMEM((3, 32, 32, 3 * FOURTH), bf16),
            pltpu.VMEM((9, 144, 512), bf16),
            pltpu.VMEM((8, 192, 512), bf16),
            pltpu.VMEM((10, 6, QB, 512), bf16),
            pltpu.VMEM((8, 4, QB, 256), bf16),
            pltpu.VMEM((8, 4, QB, 256), bf16),
            pltpu.VMEM((4, 4, QB, 256), bf16),
            pltpu.VMEM((4, 4, QB, 256), bf16),
            pltpu.VMEM((8, 4, QB, 512), bf16),
            pltpu.VMEM((8, QB, 2048), bf16),
            pltpu.VMEM((384, 1024), bf16),
            pltpu.VMEM((4, 2, QB, 512), bf16),
            pltpu.VMEM((4, 4, QB, 1024), bf16),
            pltpu.VMEM((4, 2, QB, 512), bf16),
            pltpu.VMEM((384, 1024), bf16),
            pltpu.VMEM((8, 4, QB, 512), bf16),
            pltpu.VMEM((4, 192, 512), bf16),
            pltpu.VMEM((6, 6, QB, 512), bf16),
            pltpu.SemaphoreType.DMA((3, 4)),
            pltpu.SemaphoreType.DMA((3, 5)),
            pltpu.SemaphoreType.DMA((3, 2, 5)),
            pltpu.SemaphoreType.DMA((3, 2, 5)),
            pltpu.SemaphoreType.DMA((3, 2)),
            pltpu.SemaphoreType.DMA((3, 2)),
            pltpu.SemaphoreType.DMA((3, 2)),
            pltpu.SemaphoreType.DMA((33,)),
            pltpu.SemaphoreType.DMA((33,)),
        ],
        compiler_params=pltpu.CompilerParams(
            collective_id=0, has_side_effects=True, vmem_limit_bytes=56 * 2**20
        ),
    )(tokens.reshape(576, 512), row(gain_down), qkv_down, out_down, row(merge_gain), row(gain_mid),
      row(gain_up), qkv_up, out_up, *orders(), *weights)
    return out.reshape(tokens.shape)


def solution(mesh):
    return jax.shard_map(
        on_device,
        mesh=mesh,
        in_specs=(
            P("lat", "lon", None, None), P(), P(), P(), P(), P("lon", None), P(), P("lon", None),
            P("lon", None), P("lon", None), P(), P(), P(),
        ),
        out_specs=P("lat", "lon", None, None),
        check_vma=False,
    )
```

```python
import jax
import jax.numpy as jnp
import numpy as np
from jax import lax
from jax.experimental import pallas as pl
from jax.experimental.pallas import tpu as pltpu
from jax.sharding import PartitionSpec as P

MESH = pl.DeviceIdType.MESH


def places():
    lat, lon = lax.axis_index("lat"), lax.axis_index("lon")
    lats = lax.axis_size("lat")
    core = lon % 2
    y = (lon // 2) % 8
    plane = lon // 16
    x = lat % 4
    at = lambda p, yy: p * 16 + ((yy + 16) % 8) * 2 + core
    return dict(
        north_pole=lat == 0, south_pole=lat == lats - 1,
        north=((lat + lats - 1) % lats, lon), south=((lat + 1) % lats, lon),
        beyond=((lat + 4) % lats, lon), behind=((lat + lats - 4) % lats, lon),
        west=(lat, (lon + 31) % 32), east=(lat, (lon + 1) % 32),
        lat=lat, lon=lon, core=core, x=x, y=y, plane=plane, at=at,
        up=(lat, at(plane, y + 1)),
        down=(lat, at(plane, y - 1)),
        above=((lat + 4 * plane) % lats, at(1 - plane, y)),
        below=((lat + 4 * plane + lats - 4) % lats, at(1 - plane, y)),
        right=(lat - x + (x + 1) % 4, lon),
        left=(lat - x + (x + 3) % 4, lon),
        twin=(lat, lon + 1 - 2 * core),
    )


WHOLE, FOURTH = 1024, 256


class Gather:
    def __init__(self, here, groups, near, far, ring, cross, side, second, twin, sent, local):
        self.here, self.groups, self.near, self.far = here, groups, near, far
        self.ring, self.cross, self.side, self.second = ring, cross, side, second
        self.twin, self.sent, self.local = twin, sent, local

    def push(self, src, dst, sem, to, kind=0):
        pltpu.make_async_remote_copy(
            src_ref=src, dst_ref=dst, send_sem=self.sent.at[kind], recv_sem=sem,
            device_id=self.here[to], device_id_type=MESH,
        ).start()

    def await_near(self, sem, count):
        view = self.near.at[self.groups, pl.ds(0, count)]
        pltpu.make_async_copy(view, view, sem).wait()

    def await_far(self, sem, count, fourths):
        view = self.far.at[self.groups, pl.ds(0, count), :, pl.ds(0, fourths * FOURTH)]
        pltpu.make_async_copy(view, view, sem).wait()

    def block(self, index, half=None):
        rows = slice(None) if half is None else pl.ds(16 * half, 16)
        return self.near.at[self.groups, index, rows]

    def fourth(self, index, distance, half=None):
        rows = slice(None) if half is None else pl.ds(16 * half, 16)
        if distance == 0:
            return self.near.at[self.groups, index, rows, pl.ds(WHOLE, FOURTH)]
        return self.far.at[self.groups, index, rows, pl.ds((distance - 1) * FOURTH, FOURTH)]

    def move(self, index, sem, to, half=None):
        self.push(self.block(index, half), self.block(index, half), sem, to)

    def batch(self, plane, k):
        at, y = self.here["at"], self.here["y"]
        p = self.here["plane"] if plane == 0 else 1 - self.here["plane"]
        return [at(p, y + k)] if k in (0, 4) else [at(p, y - k), at(p, y + k)]

    def spread(self, plane, k):
        blocks = self.batch(plane, k)
        if (plane, k) != (0, 0):
            for index in blocks:
                self.push(self.fourth(index, 0), self.fourth(index, 3), self.side.at[plane, k], "right", 1)
                self.push(self.fourth(index, 0), self.fourth(index, 1), self.side.at[plane, k], "left", 1)
        for index in blocks:
            self.move(index, self.twin.at[0], "twin")

    def ring_step(self, k):
        blocks = self.batch(0, k)
        if k == 0:
            self.await_near(self.local.at[0], 1)
        else:
            self.await_near(self.ring.at[k - 1], len(blocks))
        if k <= 3:
            self.move(blocks[0], self.ring.at[k], "up", 0 if k == 3 else None)
            self.move(blocks[-1], self.ring.at[k], "down", 1 if k == 3 else None)
        for index in blocks:
            self.move(index, self.cross.at[k], "above", 0)
            self.move(index, self.cross.at[k], "below", 1)
        self.spread(0, k)

    def cross_step(self, k):
        self.await_near(self.cross.at[k], len(self.batch(1, k)))
        self.spread(1, k)

    def side_step(self, plane, k):
        blocks = self.batch(plane, k)
        self.await_far(self.side.at[plane, k], len(blocks), 2)
        sem = self.second.at[plane, k]
        halves = (0, 1) if len(blocks) == 1 else (None, None)
        self.push(self.fourth(blocks[0], 3, halves[0]), self.fourth(blocks[0], 2, halves[0]), sem, "right", 1)
        self.push(self.fourth(blocks[-1], 1, halves[1]), self.fourth(blocks[-1], 2, halves[1]), sem, "left", 1)

    def last_step(self, plane, k):
        blocks = self.batch(plane, k)
        if (plane, k) == (0, 0):
            self.await_far(self.local.at[1], 1, 3)
        else:
            self.await_far(self.second.at[plane, k], len(blocks), 1)
        for index in blocks:
            view = self.far.at[self.groups, index]
            self.push(view, view, self.twin.at[1], "twin", 1)

    def settle(self):
        self.await_near(self.twin.at[0], 16)
        self.await_far(self.twin.at[1], 16, 3)

    def finish(self):
        self.await_near(self.sent.at[0], 31)
        self.await_far(self.sent.at[1], 31, 3)


def stage_own(here, owns, near, far, local):
    merge, qkv, out, expand = owns
    me, x = here["lon"], here["x"]

    def put(src, dst, sem):
        pltpu.make_async_copy(src, dst, sem).start()

    for half in range(2):
        rows = pl.ds(32 * half, 32)
        put(merge.at[rows, pl.ds(0, 512)], near.at[0, me, :, pl.ds(512 * half, 512)], local.at[0, 0])
        put(out.at[:, pl.ds(512 * half, 512)], near.at[1, me, pl.ds(16 * half, 16), pl.ds(512, 512)], local.at[1, 0])
    put(qkv.at[:, pl.ds(0, 512)], near.at[1, me, :, pl.ds(0, 512)], local.at[1, 0])
    put(expand.at[:, pl.ds(0, 1024)], near.at[2, me, :, pl.ds(0, 1024)], local.at[2, 0])
    for distance in range(4):
        fourth = (x + distance) % 4
        hold, base, sem = (near, WHOLE, 0) if distance == 0 else (far, (distance - 1) * FOURTH, 1)
        for half in range(2):
            src = merge.at[pl.ds(32 * half, 32), pl.ds(pl.multiple_of(512 + 128 * fourth, 128), 128)]
            put(src, hold.at[0, me, :, pl.ds(base + 128 * half, 128)], local.at[0, sem])
        src = qkv.at[:, pl.ds(pl.multiple_of(512 + 256 * fourth, 256), 256)]
        put(src, hold.at[1, me, :, pl.ds(base, 256)], local.at[1, sem])
        src = expand.at[:, pl.ds(pl.multiple_of(1024 + 256 * fourth, 256), 256)]
        put(src, hold.at[2, me, :, pl.ds(base, 256)], local.at[2, sem])


ORDER = (
    (0, 0, 0, 0), (0, 0, 0, 1), (0, 0, 0, 2), (3, 0, 0, 0), (3, 0, 0, 1), (3, 0, 0, 2), (1, 1, 0, 0), (1, 1, 0, 1),
    (0, 0, 1, 0), (1, 1, 0, 2), (0, 0, 1, 1), (2, 1, 0, 0), (0, 0, 1, 2), (2, 1, 0, 1), (2, 0, 1, 0), (2, 1, 0, 2),
    (1, 1, 1, 0), (0, 0, 2, 0), (2, 0, 1, 1), (3, 1, 0, 0), (1, 1, 1, 1), (0, 0, 2, 1), (2, 0, 1, 2), (3, 1, 0, 1),
    (3, 0, 1, 0), (3, 1, 0, 2), (1, 1, 1, 2), (0, 0, 2, 2), (2, 1, 1, 0), (2, 0, 2, 0), (3, 0, 1, 1), (1, 1, 2, 0),
    (0, 0, 3, 0), (2, 1, 1, 1), (2, 0, 2, 1), (3, 0, 1, 2), (1, 1, 2, 1), (0, 0, 3, 1), (2, 1, 1, 2), (2, 0, 2, 2),
    (3, 1, 1, 0), (1, 1, 2, 2), (0, 0, 3, 2), (3, 0, 2, 0), (2, 1, 2, 0), (0, 0, 4, 0), (2, 0, 3, 0), (3, 1, 1, 1),
    (1, 1, 3, 0), (3, 0, 2, 1), (0, 0, 4, 1), (2, 1, 2, 1), (2, 0, 3, 1), (1, 1, 3, 1), (3, 1, 1, 2), (3, 0, 2, 2),
    (0, 0, 4, 2), (2, 1, 2, 2), (1, 1, 3, 2), (2, 0, 3, 2), (3, 1, 2, 0), (1, 1, 4, 0), (2, 0, 4, 0), (3, 0, 3, 0),
    (1, 1, 4, 1), (2, 1, 3, 0), (2, 0, 4, 1), (3, 1, 2, 1), (3, 0, 3, 1), (1, 1, 4, 2), (2, 1, 3, 1), (2, 0, 4, 2),
    (3, 1, 2, 2), (2, 1, 3, 2), (3, 0, 3, 2), (2, 1, 4, 0), (3, 0, 4, 0), (2, 1, 4, 1), (3, 1, 3, 0), (3, 0, 4, 1),
    (2, 1, 4, 2), (3, 1, 3, 1), (3, 0, 4, 2), (3, 1, 3, 2), (3, 1, 4, 0), (3, 1, 4, 1), (3, 1, 4, 2),
)


HEADS = 4
QB = 48
GROUP = 4 * 64


def one_hot(index, width):
    out = np.zeros((len(index), width), np.float32)
    rows = np.arange(len(index))[index >= 0]
    out[rows, index[index >= 0]] = 1
    return out


def orders():
    k = np.arange(QB)
    row, col, level = k // 12, k % 12 // 2, k % 2
    valid = k < 36
    quarters = np.concatenate([np.where(valid, row * 48 + (6 * j + col) * 2 + level, -1) for j in range(4)])
    slots = []
    for slot in range(4):
        r, c = 2 * row + slot % 2, 2 * col + slot // 2
        place = (r // 3 * 2 + c // 6) * QB + r % 3 * 12 + c % 6 * 2 + level
        slots.append(np.where(valid, place, -1))
    to_quarters = one_hot(quarters, 144)
    to_merged = one_hot(np.concatenate(slots), 4 * QB)
    return [jnp.asarray(m, jnp.bfloat16) for m in (to_quarters, to_quarters.T.copy(), to_merged, to_merged.T.copy())]


def dot(a, b):
    return jnp.dot(a, b, preferred_element_type=jnp.float32)


def normed(values, gain):
    center = jnp.mean(values, axis=-1, keepdims=True)
    away = values - center
    spread = jnp.mean(away * away, axis=-1, keepdims=True)
    return (away * lax.rsqrt(spread + 1e-05) * gain).astype(jnp.bfloat16)


def attend(q, k, v, bias):
    rows = q.shape[0]
    lane = lax.broadcasted_iota(jnp.int32, (1, GROUP), 1)
    of_head = [(lane >= 64 * h) & (lane < 64 * h + 64) for h in range(HEADS)]
    stacked = jnp.concatenate([jnp.where(m, q, jnp.zeros_like(q)) for m in of_head], axis=0)
    scores = lax.dot_general(stacked, k, (((1,), (1,)), ((), ())), preferred_element_type=jnp.float32)
    scores = scores + bias
    top = jnp.max(scores, axis=-1, keepdims=True)
    weights = jnp.exp(scores - top)
    total = jnp.sum(weights, axis=-1, keepdims=True)
    mixed = dot(weights.astype(jnp.bfloat16), v) / total
    out = mixed[:rows]
    for h in range(1, HEADS):
        out = jnp.where(of_head[h], mixed[h * rows : (h + 1) * rows], out)
    return out.astype(jnp.bfloat16)


def key_bias(first_hidden, second_hidden):
    lane = lax.broadcasted_iota(jnp.int32, (1, 4 * QB), 1)
    inner = lane
    for edge in (1, 2, 3):
        inner = inner - jnp.where(lane >= edge * QB, QB, 0)
    hidden = inner >= 36
    if first_hidden is not None:
        hidden = hidden | ((lane < 2 * QB) & first_hidden)
    if second_hidden is not None:
        hidden = hidden | ((lane >= 2 * QB) & second_hidden)
    return jnp.where(hidden, jnp.float32(-1e30), jnp.float32(0))


RELAY = 30
PAUSES = (6, 9, 15, 25, 36, 48, 64)


def window_span(w, n):
    return slice(max(2 * w - 1, 0), min(2 * w + 1, n))


def attend_window(here, q, kv, att, wi, wj, rows, groups, first, last):
    inner = q.shape[3]
    cols = window_span(wj, q.shape[1])
    bias = key_bias(here["north_pole"] if first else None, here["south_pole"] if last else None)
    for g in range(groups):
        lanes = slice(g * GROUP, g * GROUP + GROUP)
        vlanes = slice(inner + g * GROUP, inner + g * GROUP + GROUP)
        queries = q[rows, cols, :, lanes]
        out = attend(
            queries.reshape(-1, GROUP),
            kv[2 * wi : 2 * wi + 2, 2 * wj : 2 * wj + 2, :, lanes].reshape(-1, GROUP),
            kv[2 * wi : 2 * wi + 2, 2 * wj : 2 * wj + 2, :, vlanes].reshape(-1, GROUP),
            bias,
        )
        att[rows, cols, :, lanes] = out.reshape(queries.shape)


def kernel(*refs):
    (tokens, gain_down, qkv_down, out_down, merge_gain, gain_mid, gain_up, qkv_up, out_up,
     to_quarters, from_quarters, to_merged, from_merged) = refs[:13]
    owns = refs[13:17]
    result = refs[17]
    near, far = refs[18:20]
    (token_rows, x_down, kv_down, q_down, att_down, q_fine, att_fine, fine_ext, merged, x_mid,
     q_mid, kv_mid, att_mid, coarse_out, expanded, joined, kv_up) = refs[20:37]
    ring, cross, side, second, twin, sent, local, halo_send, halo_recv = refs[37:]
    here = places()
    barrier = pltpu.get_barrier_semaphore()
    greeted = [here[to] for to in ("up", "down", "above", "below", "right", "left", "twin")]
    greeted += [here[to] for to in ("north", "south", "west", "east", "beyond", "behind")]
    for to in greeted:
        pl.semaphore_signal(barrier, inc=1, device_id=to, device_id_type=MESH)
    stage_own(here, owns, near, far, local)
    pl.semaphore_wait(barrier, len(greeted))
    gathers = [
        Gather(here, pl.ds(i, 1), near, far,
               *(s.at[i] for s in (ring, cross, side, second, twin, sent, local)))
        for i in range(3)
    ]
    done = [0]

    def move(until):
        for kind, plane, k, group in ORDER[done[0] : until]:
            g = gathers[group]
            if kind == 0:
                g.ring_step(k)
            elif kind == 1:
                g.cross_step(k)
            elif kind == 2:
                g.side_step(plane, k)
            else:
                g.last_step(plane, k)
        done[0] = max(done[0], until)

    copies = []

    def copy(src, dst, to):
        index = len(copies)
        copies.append(pltpu.make_async_remote_copy(
            src_ref=src, dst_ref=dst, send_sem=halo_send.at[index], recv_sem=halo_recv.at[index],
            device_id=here[to], device_id_type=MESH,
        ))
        return copies[-1]

    def columns(kv, rows):
        n = kv.shape[1] - 2
        return [
            copy(kv.at[rows, pl.ds(1, 1)], kv.at[rows, pl.ds(n + 1, 1)], "west"),
            copy(kv.at[rows, pl.ds(n, 1)], kv.at[rows, pl.ds(0, 1)], "east"),
        ]

    def start(group):
        for c in group:
            c.start()

    def wait(group):
        for c in group:
            c.wait_recv()

    def token_copies(near_by):
        both = []
        for chunk, slot, to, edge, turn in (
            (near_by, 3 + near_by, "north", 0, "left"), (3 - near_by, 2 - near_by, "south", 3, "right")
        ):
            detour = (here["x"] == edge) & (here["core"] == 1)
            index = len(copies)
            copies.append(pltpu.make_async_remote_copy(
                src_ref=tokens.at[pl.ds(144 * chunk, 144)],
                dst_ref=token_rows.at[jnp.where(detour, 6 + near_by, slot)],
                send_sem=halo_send.at[index],
                recv_sem=halo_recv.at[jnp.where(detour, RELAY + near_by, index)],
                device_id=(jnp.where(detour, here[turn][0], here[to][0]), here["lon"]),
                device_id_type=MESH,
            ))
            both.append(copies[-1])
        return both

    def relay(i, begin):
        for edge, slot, index, to in ((0, 2 - i, 2 * i + 1, "beyond"), (3, 3 + i, 2 * i, "behind")):
            @pl.when((here["x"] == edge) & (here["core"] == 1))
            def _():
                c = pltpu.make_async_remote_copy(
                    src_ref=token_rows.at[6 + i], dst_ref=token_rows.at[slot],
                    send_sem=halo_send.at[RELAY + i], recv_sem=halo_recv.at[index],
                    device_id=here[to], device_id_type=MESH,
                )
                if begin:
                    view = token_rows.at[6 + i]
                    pltpu.make_async_copy(view, view, halo_recv.at[RELAY + i]).wait()
                    c.start()
                else:
                    c.wait_send()

    token_halo = [token_copies(i) for i in range(3)]
    down_sides = columns(kv_down, pl.ds(3, 4))
    down_corners = [columns(kv_down, pl.ds(2 - i, 1)) + columns(kv_down, pl.ds(7 + i, 1)) for i in range(3)]
    mid_sides = [columns(kv_mid, pl.ds(2 * i, 2)) for i in range(2)]
    up_sides = [columns(kv_up, pl.ds(2 * i, 2)) for i in range(3)]
    bf16 = jnp.bfloat16

    def down_project(row, source):
        x = dot(to_quarters[...], source)
        n = normed(x, gain_down[...])
        if 0 < row < 9:
            x_down[row - 1] = x.astype(bf16)
            out = dot(n, qkv_down[...])
            q_down[row - 1] = (out[:, :256] * 0.125).astype(bf16).reshape(4, QB, 256)
            out = out[:, 256:]
        else:
            out = dot(n, qkv_down[:, 256:])
        kv_down[row, 1:5] = out.astype(bf16).reshape(4, QB, 512)

    def down_borders(i):
        for slot, index in ((3 + i, 2 * i), (2 - i, 2 * i + 1)):
            view = token_rows.at[slot]
            pltpu.make_async_copy(view, view, halo_recv.at[index]).wait()
        down_project(2 - i, token_rows[2 - i])
        down_project(7 + i, token_rows[3 + i])
        start(down_corners[i])

    def down_window(wi):
        for wj in (1, 0, 2):
            attend_window(here, q_down, kv_down, att_down, wi, wj, window_span(wi, 8), 1, wi == 1, wi == 3)

    def down_output(i):
        branch = dot(att_down[i].reshape(192, 256), out_down[...])
        fine_ext[i] = (x_down[i].astype(jnp.float32) + branch).astype(bf16).reshape(4, QB, 512)

    def fine_window(kv, wi, wj):
        attend_window(here, q_fine, kv, att_fine, wi, wj, window_span(wi, 4), 1, wi == 0, wi == 2)

    def merge_rows(i):
        for j in range(2):
            quad = fine_ext[2 * i : 2 * i + 2, 2 * j : 2 * j + 2].reshape(192, 512)
            spots = dot(to_merged[...], quad)
            parts = [spots[QB * k : QB * k + QB] for k in range(4)]
            center = sum(jnp.sum(p, axis=-1, keepdims=True) for p in parts) * (1 / 2048)
            parts = [p - center for p in parts]
            spread = sum(jnp.sum(p * p, axis=-1, keepdims=True) for p in parts) * (1 / 2048)
            factor = lax.rsqrt(spread + 1e-05)
            for k in range(4):
                lanes = slice(512 * k, 512 * k + 512)
                merged[2 * i + j, :, lanes] = (parts[k] * factor * merge_gain[:, lanes]).astype(bf16)

    start(token_halo[0])
    move(2)
    start(token_halo[1])
    for i in range(4):
        down_project(i + 3, tokens[144 * i : 144 * i + 144])
    start(down_sides)
    move(PAUSES[0])
    start(token_halo[2])
    relay(0, True)
    move(PAUSES[1])
    wait(down_sides)
    down_window(2)
    relay(1, True)
    move(PAUSES[2])
    down_borders(0)
    relay(2, True)
    move(PAUSES[3])
    wait(down_corners[0])
    down_window(1)
    down_window(3)
    for i in range(1, 7):
        down_output(i)
    move(PAUSES[4])
    down_borders(1)
    merge_rows(1)
    merge_rows(2)
    move(PAUSES[5])
    down_borders(2)
    move(PAUSES[6])
    wait(down_corners[1])
    wait(down_corners[2])
    down_window(0)
    down_window(4)
    down_output(0)
    down_output(7)
    merge_rows(0)
    merge_rows(3)
    move(len(ORDER))
    fourths = [(here["x"] + d) % 4 for d in range(4)]

    def held(group, d):
        return near[group, :, :, WHOLE:] if d == 0 else far[group, :, :, 256 * (d - 1) : 256 * d]

    gathers[0].settle()
    n_merged = merged[...].reshape(384, 2048)
    weight = jnp.stack([near[0, :, :, :512], near[0, :, :, 512:1024]], axis=1).reshape(2048, 512)
    x_mid[:, :512] = dot(n_merged, weight).astype(bf16)
    for d in range(4):
        hold = held(0, d)
        weight = jnp.stack([hold[:, :, :128], hold[:, :, 128:]], axis=1).reshape(2048, 128)
        lanes = pl.ds(pl.multiple_of(512 + 128 * fourths[d], 128), 128)
        x_mid[:, lanes] = dot(n_merged, weight).astype(bf16)
    n_mid = normed(x_mid[...].astype(jnp.float32), gain_mid[...])
    gathers[1].settle()
    for half in range(2):
        for d in range(4):
            out = dot(n_mid[192 * half : 192 * half + 192], held(1, d).reshape(1024, 256))
            lanes = pl.ds(pl.multiple_of(256 * fourths[d], 256), 256)
            kv_mid[2 * half : 2 * half + 2, 1:3, :, lanes] = out.astype(bf16).reshape(2, 2, QB, 256)
        start(mid_sides[half])
    out = dot(n_mid, near[1, :, :, :512].reshape(1024, 512)) * 0.125
    q_mid[...] = out.astype(bf16).reshape(4, 2, QB, 512)
    for wi in range(2):
        wait(mid_sides[wi])
        for wj in range(2):
            attend_window(here, q_mid, kv_mid, att_mid, wi, wj, slice(2 * wi, 2 * wi + 2), 2, wi == 0, wi == 1)
    for c in range(2):
        lanes = slice(512 * c, 512 * c + 512)
        weight = near[1, :, 16 * c : 16 * c + 16, 512:1024].reshape(512, 512)
        out = dot(att_mid[...].reshape(384, 512), weight)
        coarse_out[:, lanes] = (x_mid[:, lanes].astype(jnp.float32) + out).astype(bf16)
    gathers[2].settle()
    for k in range(2):
        out = dot(coarse_out[...], near[2, :, :, 512 * k : 512 * k + 512].reshape(1024, 512))
        expanded[:, k] = out.astype(bf16).reshape(8, QB, 512)
    for d in range(4):
        out = dot(coarse_out[...], held(2, d).reshape(1024, 256))
        lanes = pl.ds(pl.multiple_of(256 * (fourths[d] % 2), 256), 256)
        expanded[:, 2 + fourths[d] // 2, :, lanes] = out.astype(bf16).reshape(8, QB, 256)
    for row in range(1, 7):
        half = row % 2
        pick = from_merged[96 * half : 96 * half + 96]
        pieces = []
        for j in range(2):
            grown = dot(pick, expanded[2 * (row // 2) + j].reshape(192, 512))
            pieces.append(grown + fine_ext[row, 2 * j : 2 * j + 2].reshape(96, 512).astype(jnp.float32))
        x = jnp.concatenate(pieces, axis=0).astype(bf16)
        n = normed(x.astype(jnp.float32), gain_up[...])
        if 1 < row < 6:
            joined[row - 2] = x
            out = dot(n, qkv_up[...])
            q_fine[row - 2] = (out[:, :256] * 0.125).astype(bf16).reshape(4, QB, 256)
            out = out[:, 256:]
        else:
            out = dot(n, qkv_up[:, 256:])
        kv_up[row - 1, 1:5] = out.astype(bf16).reshape(4, QB, 512)
        if row % 2 == 0:
            start(up_sides[row // 2 - 1])
    for wi in range(3):
        fine_window(kv_up, wi, 1)
    for wi in range(3):
        wait(up_sides[wi])
        fine_window(kv_up, wi, 0)
        fine_window(kv_up, wi, 2)
    for i in range(4):
        branch = dot(att_fine[i].reshape(192, 256), out_up[...])
        out = (joined[i].astype(jnp.float32) + branch).astype(bf16)
        result[3 * i : 3 * i + 3] = dot(from_quarters[...], out).astype(bf16).reshape(3, 24, 2, 512)
    for g in gathers:
        g.finish()
    for c in copies:
        c.wait_send()
    for i in range(3):
        relay(i, False)


def on_device(tokens, gain_down, qkv_down, out_down, merge_gain, merge_weight, gain_mid, qkv_mid,
              out_mid, expand_weight, gain_up, qkv_up, out_up):
    weights = (merge_weight, qkv_mid, out_mid, expand_weight)
    row = lambda g: g.reshape(1, -1)
    bf16 = jnp.bfloat16
    vmem = pl.BlockSpec(memory_space=pltpu.VMEM)
    out = pl.pallas_call(
        kernel,
        out_shape=jax.ShapeDtypeStruct(tokens.shape, bf16),
        in_specs=[vmem] * 13 + [pl.BlockSpec(memory_space=pl.ANY)] * 4,
        out_specs=vmem,
        scratch_shapes=[
            pltpu.VMEM((3, 32, 32, WHOLE + FOURTH), bf16),
            pltpu.VMEM((3, 32, 32, 3 * FOURTH), bf16),
            pltpu.VMEM((9, 144, 512), bf16),
            pltpu.VMEM((8, 192, 512), bf16),
            pltpu.VMEM((10, 6, QB, 512), bf16),
            pltpu.VMEM((8, 4, QB, 256), bf16),
            pltpu.VMEM((8, 4, QB, 256), bf16),
            pltpu.VMEM((4, 4, QB, 256), bf16),
            pltpu.VMEM((4, 4, QB, 256), bf16),
            pltpu.VMEM((8, 4, QB, 512), bf16),
            pltpu.VMEM((8, QB, 2048), bf16),
            pltpu.VMEM((384, 1024), bf16),
            pltpu.VMEM((4, 2, QB, 512), bf16),
            pltpu.VMEM((4, 4, QB, 1024), bf16),
            pltpu.VMEM((4, 2, QB, 512), bf16),
            pltpu.VMEM((384, 1024), bf16),
            pltpu.VMEM((8, 4, QB, 512), bf16),
            pltpu.VMEM((4, 192, 512), bf16),
            pltpu.VMEM((6, 6, QB, 512), bf16),
            pltpu.SemaphoreType.DMA((3, 4)),
            pltpu.SemaphoreType.DMA((3, 5)),
            pltpu.SemaphoreType.DMA((3, 2, 5)),
            pltpu.SemaphoreType.DMA((3, 2, 5)),
            pltpu.SemaphoreType.DMA((3, 2)),
            pltpu.SemaphoreType.DMA((3, 2)),
            pltpu.SemaphoreType.DMA((3, 2)),
            pltpu.SemaphoreType.DMA((33,)),
            pltpu.SemaphoreType.DMA((33,)),
        ],
        compiler_params=pltpu.CompilerParams(
            collective_id=0, has_side_effects=True, vmem_limit_bytes=56 * 2**20
        ),
    )(tokens.reshape(576, 512), row(gain_down), qkv_down, out_down, row(merge_gain), row(gain_mid),
      row(gain_up), qkv_up, out_up, *orders(), *weights)
    return out


def solution(mesh):
    return jax.shard_map(
        on_device,
        mesh=mesh,
        in_specs=(
            P("lat", "lon", None, None), P(), P(), P(), P(), P("lon", None), P(), P("lon", None),
            P("lon", None), P("lon", None), P(), P(), P(),
        ),
        out_specs=P("lat", "lon", None, None),
        check_vma=False,
    )
```
